256 devices in a mesh: pool: 64 (over y, z, core), head: 4 (over x).
Axes of the slice: x: 4, y: 4, z: 8, core: 2. Of those that a mesh axis runs over, the one named last changes fastest.
Arguments:
- queries: bfloat16 [2048, 8192], P('pool', 'head'), may hold values from -16 to 16
- span_keys: bfloat16 [512, 512, 1024], P('pool', None, 'head'), may hold values from -7 to 7
- span_values: bfloat16 [512, 512, 1024], P('pool', None, 'head'), may hold values from -6 to 6
- span_ids: int32 [2048, 16], P('pool'), may hold values from 0 to 511, all different within a row; in each aligned block of 32 rows (0 to 31, 32 to 63, ...) at most 2 rows name the same one
- span_slot: int32 [512], replicated, may hold values from 0 to 511, each once
- out_weight: bfloat16 [8192, 5120], P('head', 'pool'), may hold values from -3 to 3
Outputs:
- mixed: bfloat16 [2048, 5120], P('pool', 'head')
The draws below stay inside these ranges and needn't reach their ends.
Inputs may be any that keep to these rules, and one draw needn't show every extreme that they name: `span_ids`: each row names 16 different spans. Within the 32 requests of one index of pool, no span is named by more than 2 requests, a bound that some block reaches. `span_slot`: each storage position appears once.
All inputs are finite; a program needn't handle non-finite values.
Results may differ from the reference program's by a relative error of at most 0.015.
Values may be sent and summed in bfloat16 or wider, within the bound.
A program may use at most 128 MiB of HBM per device.

```python
import math
import jax
import jax.numpy as jnp
import numpy as np
from jax import lax

HQ = 64
KVH = 8
HD = 128
D = 5120
CLEN = 512
TOPK = 16
REQ_DEV = 32
SPANS = 512
REQUESTS = 2048
MOST = 2


def draw_span_keys(key, part):
    key = jax.random.fold_in(key, 11)
    values = jnp.clip(jax.random.normal(key, (SPANS, CLEN, KVH * HD), jnp.float32), -4.0, 4.0)
    return values.astype(jnp.bfloat16)


def draw_queries(key, part):
    key = jax.random.fold_in(key, 12)
    first = jax.random.fold_in(key, 0)
    values = jnp.clip(jax.random.normal(first, (REQUESTS, HQ * HD), jnp.float32), -5.0, 5.0)
    values = values * 1.5
    values = jnp.clip(values, -16.0, 16.0)
    return values.astype(jnp.bfloat16)


def steps_of(stream_key, shape, cuts, low, high):
    level = 1.0
    for dim, parts in cuts:
        heights = jax.random.uniform(jax.random.fold_in(jax.random.fold_in(stream_key, 6), dim), (parts,), jnp.float32, low / len(cuts), high / len(cuts))
        level = level * jnp.repeat(jnp.exp(heights), shape[dim] // parts).reshape((-1,) + (1,) * (len(shape) - 1 - dim))
    return level


def shared_out(key, own, number, rows, amount, top, bound, slope):
    ranking = jax.random.permutation(key, amount)
    heavy_load, common = portions_of(amount, rows * top, bound, slope, True), portions_of(amount, rows * top, bound, slope, False)
    places = jnp.arange(amount)

    def named(sizes, offset_by):
        used = int((sizes > 0).sum())
        fixed = max(1, used // 4)
        shifted = fixed + (places - fixed + offset_by * (used - fixed)) % max(1, amount - fixed)
        return jnp.zeros((amount,), jnp.int32).at[ranking[jnp.where(places < fixed, places, shifted)]].set(jnp.asarray(sizes, jnp.int32))

    sizes = jnp.where(number % 4 == 0, named(heavy_load, number // 4), named(common, number - number // 4 - 1))
    mixed = jax.random.permutation(jax.random.fold_in(own, 3), amount)
    giver, taker = mixed[0:amount // 2 * 2:2], mixed[1:amount // 2 * 2:2]
    room = jnp.minimum(sizes[giver] - 1, bound - sizes[taker]) // 2
    room = jnp.where((giver == ranking[0]) | (taker == ranking[0]) | (sizes[taker] == 0), 0, jnp.maximum(room, 0))
    shifted = jax.random.randint(jax.random.fold_in(own, 4), (amount // 2,), 0, 1 << 20) % (room + 1)
    sizes = sizes.at[giver].add(-shifted).at[taker].add(shifted)
    members = jnp.searchsorted(jnp.cumsum(sizes), jnp.arange(rows * top), side="right").astype(jnp.int32)
    listing = members.reshape(top, rows).T
    listing = listing[jax.random.permutation(jax.random.fold_in(own, 1), rows)]
    offset_by = jax.random.randint(jax.random.fold_in(own, 2), (rows, 1), 0, top)
    return jnp.take_along_axis(listing, (jnp.arange(top)[None, :] + offset_by) % top, axis=1)


def portions_of(amount, total, limit, skew, full):
    loads = [(1 << 20) // math.isqrt(rank ** skew) + 1 for rank in range(1, amount + 1)]
    largest = limit if full else min(limit, max(-(-total // amount), total * loads[0] // sum(loads)))
    least = 1 if total - largest >= amount - 1 else 0
    holding, spare = [largest] + [least] * (amount - 1), total - largest - least * (amount - 1)
    while spare > 0:
        free = [i for i in range(1, amount) if holding[i] < largest] or [i for i in range(1, amount) if holding[i] < limit]
        mass, budget = sum([loads[i] for i in free]), spare
        for i in free:
            more = min(limit - holding[i], max(1, budget * loads[i] // mass), spare)
            holding[i] = holding[i] + more
            spare = spare - more
    return np.array(holding)


def noise(key, extent, width, bound, pieces=(), dtype=jnp.bfloat16):
    level = steps_of(key, extent, pieces, -0.22, 0.18) if pieces else 1.0
    drawn = jax.random.normal(key, extent, jnp.float32) * width * level
    return jnp.minimum(jnp.maximum(drawn, -bound), bound).astype(dtype)


def setup_inputs(seed: int = 0) -> dict:
    key_list = jax.random.split(jax.random.key(seed), 7)
    queries = draw_queries(jax.random.fold_in(key_list[6], 71), 0)
    span_keys = draw_span_keys(jax.random.fold_in(key_list[6], 71), 0)
    span_values = noise(key_list[2], (SPANS, CLEN, KVH * HD), 1.0, 6.0, ((0, 64), (2, 4)))
    span_ids_keys = jax.random.split(jax.random.fold_in(key_list[3], 1), REQUESTS // REQ_DEV)
    span_ids_turns = jax.random.permutation(jax.random.fold_in(key_list[3], 3), REQUESTS // REQ_DEV)
    span_ids = jax.vmap(lambda own, number: shared_out(jax.random.fold_in(key_list[3], 2), own, number, REQ_DEV, SPANS, TOPK, MOST, 2))(span_ids_keys, span_ids_turns).reshape((REQUESTS, TOPK))
    span_slot = jax.random.permutation(key_list[4], SPANS).astype(jnp.int32)
    out_weight = noise(key_list[5], (HQ * HD, D), 0.2, 3.0, ((0, 4), (1, 64)))
    return dict(queries=queries, span_keys=span_keys, span_values=span_values, span_ids=span_ids, span_slot=span_slot, out_weight=out_weight)


def reference(queries, span_keys, span_values, span_ids, span_slot, out_weight):
    group = HQ // KVH
    scale = 1.0 / math.sqrt(HD)
    slots = span_slot[span_ids]

    def one_request(inputs):
        query_row, slot_row = inputs
        cache_keys = span_keys[slot_row].astype(jnp.float32).reshape(TOPK, CLEN, KVH, HD)
        cache_values = span_values[slot_row].astype(jnp.float32).reshape(TOPK, CLEN, KVH, HD)
        query_heads = query_row.astype(jnp.float32).reshape(KVH, group, HD)
        scores = jnp.einsum('kgd,ctkd->ckgt', query_heads, cache_keys) * scale
        peaks = lax.optimization_barrier(jnp.max(scores, axis=-1))
        expo = jnp.exp(scores - peaks[..., None])
        totals = lax.optimization_barrier(jnp.sum(expo, axis=-1))
        probs = lax.optimization_barrier(expo.astype(jnp.bfloat16)).astype(jnp.float32)
        partial_value = jnp.einsum('ckgt,ctkd->ckgd', probs, cache_values) / totals[..., None]
        partial_value = lax.optimization_barrier(partial_value.astype(jnp.bfloat16)).astype(jnp.float32)
        highest = lax.optimization_barrier(jnp.max(peaks, axis=0))
        weights = jnp.exp(peaks - highest[None]) * totals
        merged = lax.optimization_barrier(jnp.sum(weights[..., None] * partial_value, axis=0)) / lax.optimization_barrier(jnp.sum(weights, axis=0))[..., None]
        return merged.astype(jnp.bfloat16).reshape(HQ * HD)
    attention = lax.map(one_request, (queries, slots), batch_size=16)
    return jnp.dot(attention, out_weight, preferred_element_type=jnp.float32).astype(jnp.bfloat16)
```

```python
import functools
import math

import jax
import jax.numpy as jnp
from jax import lax
from jax.experimental import pallas as pl
from jax.experimental.pallas import tpu as pltpu
from jax.sharding import PartitionSpec as P

NY, NZ, NC = 4, 8, 2
HR = 16
HD = 128


def coords():
    p = lax.axis_index("pool")
    return p // (NZ * NC), (p // NC) % NZ, p % NC


def pid(y, z, c):
    return ((y % NY) * NZ + z % NZ) * NC + c


def greet(peers):
    barrier = pltpu.get_barrier_semaphore()
    for peer in peers:
        pl.semaphore_signal(barrier, inc=1, device_id={"pool": peer}, device_id_type=pl.DeviceIdType.MESH)
    pl.semaphore_wait(barrier, len(peers))


def gather_kernel(q_ref, qa_ref, qb_ref, own_sem, ay_s, ay_r, az_s, az_r, bz_s, bz_r, by_s, by_r, bf_s, bf_r, sa_s, sa_r, sb_s, sb_r):
    y, z, c = coords()
    zu, zd = (z + 1) % NZ, (z + NZ - 1) % NZ
    yu, yd = (y + 1) % NY, (y + NY - 1) % NY
    sib = pid(y, z, 1 - c)
    greet([pid(y + 1, z, c), pid(y + 2, z, c), pid(y + 3, z, c), pid(y, z + 1, c), pid(y, z + 7, c), sib])

    sends = []

    def send(src, dst, ss, rs, to):
        d = pltpu.make_async_remote_copy(src_ref=src, dst_ref=dst, send_sem=ss, recv_sem=rs, device_id={"pool": to}, device_id_type=pl.DeviceIdType.MESH)
        d.start()
        sends.append(d)

    def arrived(dst, ss, rs):
        pltpu.make_async_remote_copy(src_ref=dst, dst_ref=dst, send_sem=ss, recv_sem=rs, device_id={"pool": sib}, device_id_type=pl.DeviceIdType.MESH).wait_recv()

    qa, qb = q_ref.at[0], q_ref.at[1]
    own_a = pltpu.make_async_copy(qa, qa_ref.at[c, z, y], own_sem.at[0])
    own_b = pltpu.make_async_copy(qb, qb_ref.at[c, y, z], own_sem.at[1])
    own_a.start()
    own_b.start()

    def b_z(k):
        up = qb if k == 1 else qb_ref.at[c, y, (z + NZ - (k - 1)) % NZ]
        dn = qb if k == 1 else qb_ref.at[c, y, (z + k - 1) % NZ]
        iu, idn = (z + NZ - (k - 1)) % NZ, (z + k - 1) % NZ
        if k < 4:
            send(up, qb_ref.at[c, y, iu], bz_s.at[2 * k - 2], bz_r.at[2 * k - 2], pid(y, zu, c))
            send(dn, qb_ref.at[c, y, idn], bz_s.at[2 * k - 1], bz_r.at[2 * k - 1], pid(y, zd, c))
        else:
            lo, hi = pl.ds(0, HR // 2), pl.ds(HR // 2, HR // 2)
            send(up.at[lo], qb_ref.at[c, y, iu, lo], bz_s.at[6], bz_r.at[6], pid(y, zu, c))
            send(dn.at[hi], qb_ref.at[c, y, idn, hi], bz_s.at[7], bz_r.at[7], pid(y, zd, c))

    def b_z_wait(k):
        iu, idn = (z + NZ - k) % NZ, (z + k) % NZ
        if k < 4:
            arrived(qb_ref.at[c, y, iu], bz_s.at[2 * k - 2], bz_r.at[2 * k - 2])
            arrived(qb_ref.at[c, y, idn], bz_s.at[2 * k - 1], bz_r.at[2 * k - 1])
        else:
            lo, hi = pl.ds(0, HR // 2), pl.ds(HR // 2, HR // 2)
            arrived(qb_ref.at[c, y, iu, lo], bz_s.at[6], bz_r.at[6])
            arrived(qb_ref.at[c, y, idn, hi], bz_s.at[7], bz_r.at[7])

    offs = [0, NZ - 1, 1, NZ - 2, 2, NZ - 3, 3, 4]

    def b_y(i):
        zz = (z + offs[i]) % NZ
        src = qb if i == 0 else qb_ref.at[c, y, zz]
        send(src, qb_ref.at[c, y, zz], by_s.at[2 * i], by_r.at[2 * i], pid(yu, z, c))
        send(src, qb_ref.at[c, y, zz], by_s.at[2 * i + 1], by_r.at[2 * i + 1], pid(yd, z, c))

    def b_f(i):
        zz = (z + offs[i]) % NZ
        arrived(qb_ref.at[c, yd, zz], by_s.at[2 * i], by_r.at[2 * i])
        arrived(qb_ref.at[c, yu, zz], by_s.at[2 * i + 1], by_r.at[2 * i + 1])
        lo, hi = pl.ds(0, HR // 2), pl.ds(HR // 2, HR // 2)
        send(qb_ref.at[c, yd, zz, lo], qb_ref.at[c, yd, zz, lo], bf_s.at[2 * i], bf_r.at[2 * i], pid(yu, z, c))
        send(qb_ref.at[c, yu, zz, hi], qb_ref.at[c, yu, zz, hi], bf_s.at[2 * i + 1], bf_r.at[2 * i + 1], pid(yd, z, c))

    def b_f_wait(i):
        zz = (z + offs[i]) % NZ
        lo, hi = pl.ds(0, HR // 2), pl.ds(HR // 2, HR // 2)
        yo = (y + 2) % NY
        arrived(qb_ref.at[c, yo, zz, lo], bf_s.at[2 * i], bf_r.at[2 * i])
        arrived(qb_ref.at[c, yo, zz, hi], bf_s.at[2 * i + 1], bf_r.at[2 * i + 1])

    jo = [0, 1, 3, 2]

    def a_z(k, j):
        yy = (y + jo[j]) % NY
        iu, idn = (z + NZ - (k - 1)) % NZ, (z + k - 1) % NZ
        up = qa if k == 1 and j == 0 else qa_ref.at[c, iu, yy]
        dn = qa if k == 1 and j == 0 else qa_ref.at[c, idn, yy]
        n = 8 * (k - 1) + 2 * j
        if k < 4 or j % 2 == 0:
            send(up, qa_ref.at[c, iu, yy], az_s.at[n], az_r.at[n], pid(y, zu, c))
        if k < 4 or j % 2 == 1:
            send(dn, qa_ref.at[c, idn, yy], az_s.at[n + 1], az_r.at[n + 1], pid(y, zd, c))

    def a_z_wait(k, j):
        yy = (y + jo[j]) % NY
        n = 8 * (k - 1) + 2 * j
        if k < 4 or j % 2 == 0:
            arrived(qa_ref.at[c, (z + NZ - k) % NZ, yy], az_s.at[n], az_r.at[n])
        if k < 4 or j % 2 == 1:
            arrived(qa_ref.at[c, (z + k) % NZ, yy], az_s.at[n + 1], az_r.at[n + 1])

    def s_a(i):
        zz = (z + offs[i]) % NZ
        send(qa_ref.at[c, zz], qa_ref.at[c, zz], sa_s.at[i], sa_r.at[i], sib)

    def s_b(j):
        yy = (y + j) % NY
        send(qb_ref.at[c, yy], qb_ref.at[c, yy], sb_s.at[j], sb_r.at[j], sib)

    b_z(1)
    for d in (1, 3, 2):
        send(qa, qa_ref.at[c, z, y], ay_s.at[d - 1], ay_r.at[d - 1], pid(y + d, z, c))
    a_z(1, 0)
    b_y(0)
    b_z_wait(1)
    b_z(2)
    b_y(1)
    b_y(2)
    for j in (1, 2, 3):
        d = (NY - jo[j]) % NY
        arrived(qa_ref.at[c, z, (y + jo[j]) % NY], ay_s.at[d - 1], ay_r.at[d - 1])
        a_z(1, j)
    own_a.wait()
    own_b.wait()
    s_a(0)
    b_f(0)
    for k in (1, 2, 3):
        b_z_wait(k + 1)
        if k < 3:
            b_z(k + 2)
        b_y(2 * k + 1)
        if k < 3:
            b_y(2 * k + 2)
        for j in range(4):
            a_z_wait(k, j)
            a_z(k + 1, j)
            if j == 1:
                b_f(2 * k - 1)
            if j == 3:
                b_f(2 * k)
        s_a(2 * k - 1)
        s_a(2 * k)
        if k == 3:
            s_b(0)
    b_f(7)
    s_b(1)
    s_b(3)
    for i in range(8):
        b_f_wait(i)
    s_b(2)
    for j in range(4):
        a_z_wait(4, j)
    s_a(7)
    for i in range(8):
        arrived(qa_ref.at[1 - c, (z + offs[i]) % NZ], sa_s.at[i], sa_r.at[i])
    for j in range(4):
        arrived(qb_ref.at[1 - c, (y + j) % NY], sb_s.at[j], sb_r.at[j])
    for d in sends:
        d.wait_send()


def gather_queries(q):
    dma = pltpu.SemaphoreType.DMA
    heads, hd = q.shape[1], q.shape[2]
    return pl.pallas_call(
        gather_kernel,
        out_shape=(
            jax.ShapeDtypeStruct((NC, NZ, NY, HR, heads, hd), q.dtype),
            jax.ShapeDtypeStruct((NC, NY, NZ, HR, heads, hd), q.dtype),
        ),
        in_specs=[pl.BlockSpec(memory_space=pl.ANY)],
        out_specs=(pl.BlockSpec(memory_space=pl.ANY),) * 2,
        scratch_shapes=[dma((2,)), dma((3,)), dma((3,)), dma((32,)), dma((32,)), dma((8,)), dma((8,)), dma((16,)), dma((16,)), dma((16,)), dma((16,)), dma((8,)), dma((8,)), dma((4,)), dma((4,))],
        compiler_params=pltpu.CompilerParams(collective_id=0, has_side_effects=True),
        name="gather_queries",
    )(q.reshape(2, HR, heads, hd))


NEG = -1e30
CHUNK = 32
ROWS = 2048
FLAG = 4096


def span_lists(ids_all, span_slot, local_spans):
    picks = ids_all.shape[-1]
    me = lax.axis_index("pool")
    mine = me * local_spans + jnp.arange(local_spans, dtype=jnp.int32)
    hit = span_slot[None, :] == mine[:, None]
    names = jnp.sum(jnp.where(hit, jnp.arange(span_slot.shape[0], dtype=jnp.int32)[None, :], 0), axis=1)
    member = jnp.any(ids_all[None] == names[:, None, None], axis=2).astype(jnp.float32)
    m = member.reshape(local_spans, NY, NZ, NC, 2, HR)
    first = m[:, :, :, :, 0].transpose(0, 3, 2, 1, 4).reshape(local_spans, -1)
    second = m[:, :, :, :, 1].transpose(0, 3, 1, 2, 4).reshape(local_spans, -1)
    m = jnp.concatenate([first, second], axis=1)
    parts = m.reshape(local_spans, ROWS // 128, 128)
    lane = jnp.arange(128)
    before = (lane[:, None] < lane[None, :]).astype(jnp.float32)
    within = jnp.einsum("sgl,lk->sgk", parts, before, preferred_element_type=jnp.float32)
    sums = jnp.sum(parts, axis=2)
    grp = jnp.arange(ROWS // 128)
    offset = jnp.sum(jnp.where(grp[None, :, None] > grp[None, None, :], sums[:, None, :], 0.0), axis=2)
    rank = (within + offset[:, :, None]).reshape(local_spans, ROWS).astype(jnp.int32)
    count = jnp.sum(sums, axis=1).astype(jnp.int32)
    span = jnp.arange(local_spans)
    prior = jnp.max(jnp.where(span[:, None, None] > span[None, :, None], m[None], 0.0), axis=1)
    place = jnp.arange(ROWS, dtype=jnp.int32)[None, :] + jnp.where(prior > 0, FLAG, 0)
    rank = jnp.where(m > 0, rank, -1)
    slot = jnp.arange(128, dtype=jnp.int32)
    listing = jnp.sum(jnp.where(rank[:, None, :] == slot[None, :, None], place[:, None, :], 0), axis=2)
    listing = jnp.where(slot[None, :] < count[:, None], listing, ROWS)
    return listing, count


def attend_kernel(list_ref, count_ref, qa_ref, qb_ref, k_ref, v_ref, da_ref, db_ref, st_ref, qbuf, dbuf, l0, l1, p0, p1, e0, e1, sem):
    s = pl.program_id(0)
    half = ROWS // 2

    @pl.when(s == 0)
    def _():
        ca = pltpu.make_async_copy(qa_ref, qbuf.at[pl.ds(0, half)], sem.at[0])
        cb = pltpu.make_async_copy(qb_ref, qbuf.at[pl.ds(half, half)], sem.at[1])
        ca.start()
        cb.start()

        def clear(i, _):
            dbuf[pl.ds(i * 16, 16)] = jnp.zeros((16, 16, 128), jnp.bfloat16)
            return 0

        lax.fori_loop(0, ROWS // 16, clear, 0)
        qbuf[pl.ds(ROWS, 8)] = jnp.zeros((8, 16, 128), jnp.bfloat16)
        st_ref[...] = jnp.full(st_ref.shape, NEG, jnp.float32)
        ca.wait()
        cb.wait()

    scale2 = math.log2(math.e) / math.sqrt(HD)
    lane = lax.broadcasted_iota(jnp.int32, (16, 128), 1)
    n = count_ref[s]

    def group_of(place):
        in_b = place >= half
        q = place - jnp.where(in_b, half, 0)
        g = jnp.where(in_b, 16 + q // 128, q // 64)
        return g, jnp.where(in_b, q % 128, q % 64)

    def chunk(j, _):
        base = j * CHUNK
        for i in range(0, CHUNK, 2):
            a = qbuf[list_ref[s, base + i] & (FLAG - 1)].astype(jnp.float32)
            b = qbuf[list_ref[s, base + i + 1] & (FLAG - 1)].astype(jnp.float32)
            l0[pl.ds(i * 8, 16)] = jnp.concatenate([a[0:8], b[0:8]], axis=0).astype(jnp.bfloat16)
            l1[pl.ds(i * 8, 16)] = jnp.concatenate([a[8:16], b[8:16]], axis=0).astype(jnp.bfloat16)
        for kv, (l, p, e) in enumerate(((l0, p0, e0), (l1, p1, e1))):
            keys = k_ref[0, :, kv * HD:(kv + 1) * HD]
            vals = v_ref[0, :, kv * HD:(kv + 1) * HD]
            sc = lax.dot_general(l[...], keys, (((1,), (1,)), ((), ())), preferred_element_type=jnp.float32) * scale2
            m = jnp.max(sc, axis=1, keepdims=True)
            ex = jnp.exp2(sc - m)
            tot = jnp.sum(ex, axis=1, keepdims=True)
            pv = jnp.dot(ex.astype(jnp.bfloat16), vals, preferred_element_type=jnp.float32)
            p[...] = pv / tot
            e[...] = jnp.broadcast_to(m + jnp.log2(tot), e.shape)
        for i in range(CHUNK):
            entry = list_ref[s, base + i]
            place = entry & (FLAG - 1)
            fresh = entry < FLAG
            new = jnp.concatenate([p0[pl.ds(i * 8, 8)], p1[pl.ds(i * 8, 8)]], axis=0)
            dbuf[jnp.where(fresh, place, ROWS)] = new.astype(jnp.bfloat16)
            g, at = group_of(jnp.minimum(place, ROWS - 1))
            at = jnp.where((entry < ROWS), at, -1)
            le = jnp.concatenate([e0[pl.ds(i * 8, 8)], e1[pl.ds(i * 8, 8)]], axis=0)
            st_ref[g] = jnp.where(lane == at, le, st_ref[g])

        def again(i, _):
            entry = list_ref[s, base + i]

            @pl.when(entry >= FLAG)
            def _():
                place = entry & (FLAG - 1)
                g, at = group_of(place)
                new = jnp.concatenate([p0[pl.ds(pl.multiple_of(i * 8, 8), 8)], p1[pl.ds(pl.multiple_of(i * 8, 8), 8)]], axis=0)
                le = jnp.concatenate([e0[pl.ds(pl.multiple_of(i * 8, 8), 8)], e1[pl.ds(pl.multiple_of(i * 8, 8), 8)]], axis=0)
                st = st_ref[g]
                old = jnp.max(jnp.where(lane == at, st, -3e38), axis=1, keepdims=True)
                top = jnp.maximum(old, le)
                wo, wn = jnp.exp2(old - top), jnp.exp2(le - top)
                both = wo + wn
                before = dbuf[place].astype(jnp.float32)
                dbuf[place] = (before + (wn / both) * (new - before)).astype(jnp.bfloat16)
                st_ref[g] = jnp.where(lane == at, top + jnp.log2(both), st)

            return 0

        lax.fori_loop(0, jnp.minimum(n - base, CHUNK), again, 0)
        return 0

    lax.fori_loop(0, (n + CHUNK - 1) // CHUNK, chunk, 0)

    @pl.when(s == pl.num_programs(0) - 1)
    def _():
        ca = pltpu.make_async_copy(dbuf.at[pl.ds(0, half)], da_ref, sem.at[0])
        cb = pltpu.make_async_copy(dbuf.at[pl.ds(half, half)], db_ref, sem.at[1])
        ca.start()
        cb.start()
        ca.wait()
        cb.wait()


def attend(listing, count, qa, qb, span_keys, span_values):
    spans, length, width = span_keys.shape
    half = ROWS // 2
    tile = jax.ShapeDtypeStruct((half, 16, HD), jnp.bfloat16)
    block = pl.BlockSpec((1, length, width), lambda s: (s, 0, 0))
    return pl.pallas_call(
        attend_kernel,
        grid=(spans,),
        out_shape=(tile, tile, jax.ShapeDtypeStruct((24, 16, 128), jnp.float32)),
        in_specs=[
            pl.BlockSpec(memory_space=pltpu.SMEM),
            pl.BlockSpec(memory_space=pltpu.SMEM),
            pl.BlockSpec(memory_space=pl.ANY),
            pl.BlockSpec(memory_space=pl.ANY),
            block,
            block,
        ],
        out_specs=(
            pl.BlockSpec(memory_space=pl.ANY),
            pl.BlockSpec(memory_space=pl.ANY),
            pl.BlockSpec((24, 16, 128), lambda s: (0, 0, 0)),
        ),
        scratch_shapes=[
            pltpu.VMEM((ROWS + 8, 16, HD), jnp.bfloat16),
            pltpu.VMEM((ROWS + 8, 16, HD), jnp.bfloat16),
            pltpu.VMEM((CHUNK * 8, HD), jnp.bfloat16),
            pltpu.VMEM((CHUNK * 8, HD), jnp.bfloat16),
            pltpu.VMEM((CHUNK * 8, HD), jnp.float32),
            pltpu.VMEM((CHUNK * 8, HD), jnp.float32),
            pltpu.VMEM((CHUNK * 8, HD), jnp.float32),
            pltpu.VMEM((CHUNK * 8, HD), jnp.float32),
            pltpu.SemaphoreType.DMA((2,)),
        ],
        compiler_params=pltpu.CompilerParams(vmem_limit_bytes=48 * 2**20, dimension_semantics=("arbitrary",)),
        name="attend",
    )(listing, count, qa.reshape(half, 16, HD), qb.reshape(half, 16, HD), span_keys, span_values)


def merge_kernel(da_ref, db_ref, sa_ref, sb_ref, out_ref,
                 ma, mb, ra, rb, sa, sb, rsa, rsb,
                 ua, da, usa, dsa, ub, db, usb, dsb, ya, ysa, uz, dz, usz, dsz,
                 own_sem, sib_s, sib_r, ua_s, ua_r, da_s, da_r, usa_s, usa_r, dsa_s, dsa_r,
                 ub_s, ub_r, db_s, db_r, usb_s, usb_r, dsb_s, dsb_r,
                 ya_s, ya_r, ysa_s, ysa_r, uz_s, uz_r, dz_s, dz_r, usz_s, usz_r, dsz_s, dsz_r):
    y, z, c = coords()
    zup, zdn = pid(y, z + 1, c), pid(y, z + NZ - 1, c)
    yup, ydn = pid(y + 1, z, c), pid(y + NY - 1, z, c)
    sib = pid(y, z, 1 - c)
    lane = lax.broadcasted_iota(jnp.int32, (16, 128), 1)

    loads = [
        pltpu.make_async_copy(da_ref.at[c], ma, own_sem.at[0]),
        pltpu.make_async_copy(db_ref.at[c], mb, own_sem.at[1]),
        pltpu.make_async_copy(sa_ref.at[c], sa, own_sem.at[2]),
        pltpu.make_async_copy(sb_ref.at[c], sb, own_sem.at[3]),
    ]
    for d in loads:
        d.start()
    greet([pid(y + 1, z, c), pid(y + 2, z, c), pid(y + 3, z, c), zup, zdn, sib])
    sends = []

    def send(src, dst, ss, rs, to):
        d = pltpu.make_async_remote_copy(src_ref=src, dst_ref=dst, send_sem=ss, recv_sem=rs, device_id={"pool": to}, device_id_type=pl.DeviceIdType.MESH)
        d.start()
        sends.append(d)

    def arrived(dst, ss, rs):
        pltpu.make_async_remote_copy(src_ref=dst, dst_ref=dst, send_sem=ss, recv_sem=rs, device_id={"pool": sib}, device_id_type=pl.DeviceIdType.MESH).wait_recv()

    def zz(d):
        return (z + d + NZ) % NZ

    def yy(d):
        return (y + d + NY) % NY

    a_order = [4, 3, -3, 2, -2, 1, -1, 0]
    b_order = [2, 1, -1, 0]
    send(sa_ref.at[1 - c], rsa, sib_s.at[12], sib_r.at[12], sib)
    send(sb_ref.at[1 - c], rsb, sib_s.at[13], sib_r.at[13], sib)

    def sib_a(i):
        w = zz(a_order[i])
        send(da_ref.at[1 - c, w], ra.at[w], sib_s.at[i], sib_r.at[i], sib)

    def sib_b(i):
        w = yy(b_order[i])
        send(db_ref.at[1 - c, w], rb.at[w], sib_s.at[8 + i], sib_r.at[8 + i], sib)

    sib_a(0)
    sib_b(0)
    sib_a(1)
    sib_a(2)
    sib_b(1)
    sib_b(2)
    sib_a(3)
    sib_a(4)
    sib_a(5)
    sib_a(6)
    sib_b(3)
    sib_a(7)

    def blend(dst, src, wt, rows=HR, start=0):
        for i in range(start, start + rows):
            w = jnp.broadcast_to(wt[:, i:i + 1], (16, 128))
            a = dst[i].astype(jnp.float32)
            b = src[i].astype(jnp.float32)
            dst[i] = (a + w * (b - a)).astype(jnp.bfloat16)

    def join(own, other):
        top = jnp.maximum(own, other)
        low = jnp.minimum(own, other)
        new = top + jnp.log2(1.0 + jnp.exp2(low - top))
        return new, jnp.exp2(other - new)

    def turned(wt, by):
        return pltpu.roll(wt, (128 - by) % 128, 1)

    for d in loads:
        d.wait()
    arrived(rsa, sib_s.at[12], sib_r.at[12])
    arrived(rsb, sib_s.at[13], sib_r.at[13])

    def core_a(i):
        w = zz(a_order[i])
        arrived(ra.at[w], sib_s.at[i], sib_r.at[i])
        new, wt = join(sa[w], rsa[w])
        sa[w] = new

        def cell(j, wt):
            blend(ma.at[w, j], ra.at[w, j], wt)
            return pltpu.roll(wt, 128 - HR, 1)

        lax.fori_loop(0, NY, cell, wt)

    def core_b(i):
        w = yy(b_order[i])
        arrived(rb.at[w], sib_s.at[8 + i], sib_r.at[8 + i])
        new, wt = join(sb[w], rsb[w])
        sb[w] = new

        def cell(j, wt):
            blend(mb.at[w, j], rb.at[w, j], wt)
            return pltpu.roll(wt, 128 - HR, 1)

        lax.fori_loop(0, NZ, cell, wt)

    def a_first():
        w = zz(4)
        st = sa[w]
        usa[4] = jnp.where(lane < 2 * HR, st, NEG)
        dsa[4] = jnp.where(lane < 2 * HR, NEG, st)
        send(usa.at[4], usa.at[0], usa_s.at[0], usa_r.at[0], zup)
        send(dsa.at[4], dsa.at[0], dsa_s.at[0], dsa_r.at[0], zdn)
        for j in (0, 1):
            send(ma.at[w, j], ua.at[0, j], ua_s.at[j], ua_r.at[j], zup)
            send(ma.at[w, 2 + j], da.at[0, 2 + j], da_s.at[2 + j], da_r.at[2 + j], zdn)

    def a_step(k):
        wu, wd = zz(4 - k), zz(k - 4)
        arrived(usa.at[k - 1], usa_s.at[k - 1], usa_r.at[k - 1])
        newu, wtu = join(sa[wu], usa[k - 1])
        sa[wu] = newu
        if k < 4:
            send(sa.at[wu], usa.at[k], usa_s.at[k], usa_r.at[k], zup)
        arrived(dsa.at[k - 1], dsa_s.at[k - 1], dsa_r.at[k - 1])
        newd, wtd = join(sa[wd], dsa[k - 1])
        sa[wd] = newd
        if k < 4:
            send(sa.at[wd], dsa.at[k], dsa_s.at[k], dsa_r.at[k], zdn)

        for j in range(NY):
            n = 4 * (k - 1) + j
            if k > 1 or j < 2:
                arrived(ua.at[k - 1, j], ua_s.at[n], ua_r.at[n])
                blend(ma.at[wu, j], ua.at[k - 1, j], turned(wtu, HR * j))
            if k < 4:
                send(ma.at[wu, j], ua.at[k, j], ua_s.at[n + 4], ua_r.at[n + 4], zup)
            if k > 1 or j >= 2:
                arrived(da.at[k - 1, j], da_s.at[n], da_r.at[n])
                blend(ma.at[wd, j], da.at[k - 1, j], turned(wtd, HR * j))
            if k < 4:
                send(ma.at[wd, j], da.at[k, j], da_s.at[n + 4], da_r.at[n + 4], zdn)

    def b_first():
        w = yy(2)
        st = sb[w]
        usb[2] = jnp.where(lane < 4 * HR, st, NEG)
        dsb[2] = jnp.where(lane < 4 * HR, NEG, st)
        send(usb.at[2], usb.at[0], usb_s.at[0], usb_r.at[0], yup)
        send(dsb.at[2], dsb.at[0], dsb_s.at[0], dsb_r.at[0], ydn)
        for j in range(4):
            send(mb.at[w, j], ub.at[0, j], ub_s.at[j], ub_r.at[j], yup)
            send(mb.at[w, 4 + j], db.at[0, 4 + j], db_s.at[4 + j], db_r.at[4 + j], ydn)

    def b_step(k):
        wu, wd = yy(2 - k), yy(k - 2)
        arrived(usb.at[k - 1], usb_s.at[k - 1], usb_r.at[k - 1])
        newu, wtu = join(sb[wu], usb[k - 1])
        sb[wu] = newu
        if k < 2:
            send(sb.at[wu], usb.at[k], usb_s.at[k], usb_r.at[k], yup)
        arrived(dsb.at[k - 1], dsb_s.at[k - 1], dsb_r.at[k - 1])
        newd, wtd = join(sb[wd], dsb[k - 1])
        sb[wd] = newd
        if k < 2:
            send(sb.at[wd], dsb.at[k], dsb_s.at[k], dsb_r.at[k], ydn)
        for j in range(NZ):
            n = 8 * (k - 1) + j
            if k > 1 or j < 4:
                arrived(ub.at[k - 1, j], ub_s.at[n], ub_r.at[n])
                blend(mb.at[wu, j], ub.at[k - 1, j], turned(wtu, HR * j))
            if k < 2:
                send(mb.at[wu, j], ub.at[k, j], ub_s.at[n + 8], ub_r.at[n + 8], yup)
            if k > 1 or j >= 4:
                arrived(db.at[k - 1, j], db_s.at[n], db_r.at[n])
                blend(mb.at[wd, j], db.at[k - 1, j], turned(wtd, HR * j))
            if k < 2:
                send(mb.at[wd, j], db.at[k, j], db_s.at[n + 8], db_r.at[n + 8], ydn)

    def a_y():
        for d in (1, 2, 3):
            w = yy(d)
            send(sa.at[z], ysa.at[d - 1], ysa_s.at[d - 1], ysa_r.at[d - 1], pid(y + d, z, c))
            send(ma.at[z, w], ya.at[d - 1], ya_s.at[d - 1], ya_r.at[d - 1], pid(y + d, z, c))

    def a_y_end():
        total = turned(sa[z], HR * y)
        for d in (1, 3, 2):
            arrived(ysa.at[d - 1], ysa_s.at[d - 1], ysa_r.at[d - 1])
            total, wt = join(total, turned(ysa[d - 1], HR * y))
            arrived(ya.at[d - 1], ya_s.at[d - 1], ya_r.at[d - 1])
            blend(ma.at[z, y], ya.at[d - 1], wt)

    def bz_first():
        w = zz(4)
        usz[4] = turned(sb[y], HR * w)
        send(usz.at[4], usz.at[0], usz_s.at[0], usz_r.at[0], zup)
        send(usz.at[4], dsz.at[0], dsz_s.at[0], dsz_r.at[0], zdn)
        lo, hi = pl.ds(0, HR // 2), pl.ds(HR // 2, HR // 2)
        send(mb.at[y, w, lo], uz.at[0, lo], uz_s.at[0], uz_r.at[0], zup)
        send(mb.at[y, w, hi], dz.at[0, hi], dz_s.at[0], dz_r.at[0], zdn)

    def bz_step(k):
        wu, wd = zz(4 - k), zz(k - 4)
        lo, hi = pl.ds(0, HR // 2), pl.ds(HR // 2, HR // 2)
        arrived(usz.at[k - 1], usz_s.at[k - 1], usz_r.at[k - 1])
        ru = usz[k - 1]
        if k == 1:
            ru = jnp.where(lane < HR // 2, ru, NEG)
        newu, wtu = join(turned(sb[y], HR * wu), ru)
        if k < 4:
            usz[4 + k] = newu
            send(usz.at[4 + k], usz.at[k], usz_s.at[k], usz_r.at[k], zup)
        arrived(dsz.at[k - 1], dsz_s.at[k - 1], dsz_r.at[k - 1])
        rd = dsz[k - 1]
        if k == 1:
            rd = jnp.where(lane < HR // 2, NEG, rd)
        own = turned(sb[y], HR * wd) if k < 4 else newu
        newd, wtd = join(own, rd)
        if k < 4:
            dsz[4 + k] = newd
            send(dsz.at[4 + k], dsz.at[k], dsz_s.at[k], dsz_r.at[k], zdn)
        if k == 1:
            arrived(uz.at[0, lo], uz_s.at[0], uz_r.at[0])
            blend(mb.at[y, wu], uz.at[0], wtu, HR // 2, 0)
        else:
            arrived(uz.at[k - 1], uz_s.at[k - 1], uz_r.at[k - 1])
            blend(mb.at[y, wu], uz.at[k - 1], wtu)
        if k < 4:
            send(mb.at[y, wu], uz.at[k], uz_s.at[k], uz_r.at[k], zup)
        if k == 1:
            arrived(dz.at[0, hi], dz_s.at[0], dz_r.at[0])
            blend(mb.at[y, wd], dz.at[0], wtd, HR // 2, HR // 2)
        else:
            arrived(dz.at[k - 1], dz_s.at[k - 1], dz_r.at[k - 1])
            blend(mb.at[y, wd], dz.at[k - 1], wtd)
        if k < 4:
            send(mb.at[y, wd], dz.at[k], dz_s.at[k], dz_r.at[k], zdn)

    core_a(0)
    a_first()
    core_b(0)
    b_first()
    core_a(1)
    core_a(2)
    a_step(1)
    core_b(1)
    core_b(2)
    b_step(1)
    core_a(3)
    core_a(4)
    a_step(2)
    core_a(5)
    core_a(6)
    a_step(3)
    core_b(3)
    b_step(2)
    bz_first()
    core_a(7)
    a_step(4)
    a_y()
    bz_step(1)
    bz_step(2)
    a_y_end()
    bz_step(3)
    bz_step(4)
    for d in sends:
        d.wait_send()
    out_ref[pl.ds(0, HR)] = ma[z, y]
    out_ref[pl.ds(HR, HR)] = mb[y, z]


def merge(da, db, st):
    dma = pltpu.SemaphoreType.DMA
    bf, f32 = jnp.bfloat16, jnp.float32

    def v(*shape, dtype=bf):
        return pltpu.VMEM(shape + (16, 128), dtype)

    anyspec = pl.BlockSpec(memory_space=pl.ANY)
    sems = [4, 14, 14, 16, 16, 16, 16, 4, 4, 4, 4, 16, 16, 16, 16, 2, 2, 2, 2, 3, 3, 3, 3, 4, 4, 4, 4, 4, 4, 4, 4]
    return pl.pallas_call(
        merge_kernel,
        out_shape=jax.ShapeDtypeStruct((2 * HR, 16, 128), bf),
        in_specs=[anyspec] * 4,
        out_specs=pl.BlockSpec(memory_space=pltpu.VMEM),
        scratch_shapes=[
            v(NZ, NY, HR), v(NY, NZ, HR), v(NZ, NY, HR), v(NY, NZ, HR),
            v(NZ, dtype=f32), v(NY, dtype=f32), v(NZ, dtype=f32), v(NY, dtype=f32),
            v(4, NY, HR), v(4, NY, HR), v(5, dtype=f32), v(5, dtype=f32),
            v(2, NZ, HR), v(2, NZ, HR), v(3, dtype=f32), v(3, dtype=f32),
            v(3, HR), v(3, dtype=f32),
            v(4, HR), v(4, HR), v(8, dtype=f32), v(8, dtype=f32),
        ] + [dma((n,)) for n in sems],
        compiler_params=pltpu.CompilerParams(collective_id=1, has_side_effects=True, vmem_limit_bytes=40 * 2**20),
        name="merge",
    )(
        da.reshape(NC, NZ, NY, HR, 16, 128),
        db.reshape(NC, NY, NZ, HR, 16, 128),
        st[:16].reshape(NC, NZ, 16, 128),
        st[16:].reshape(NC, NY, 16, 128),
    )


def body(queries, span_keys, span_values, span_ids, span_slot, out_weight):
    rows, width = queries.shape
    ids_all = lax.all_gather(span_ids, "pool", axis=0, tiled=True)
    zc = NZ * NC
    weight = lax.all_gather(out_weight.T, "pool", axis=0, tiled=True, axis_index_groups=[[y * zc + i for i in range(zc)] for y in range(NY)])
    qa, qb = gather_queries(queries.reshape(rows, width // HD, HD))
    listing, count = span_lists(ids_all, span_slot, span_keys.shape[0])
    da, db, st = attend(listing, count, qa, qb, span_keys, span_values)
    attention = merge(da, db, st).reshape(rows, width)
    near = lax.all_gather(attention, "pool", axis=0, tiled=True, axis_index_groups=[[y * zc + i for y in range(NY)] for i in range(zc)])
    terms = lax.dot_general(near, weight, (((1,), (1,)), ((), ())), preferred_element_type=jnp.float32)
    mine = lax.psum_scatter(terms.astype(jnp.bfloat16), "head", scatter_dimension=0, tiled=True)
    perm = []
    for y in range(NY):
        for i in range(zc):
            for x in range(4):
                perm.append(((y * zc + i) * 4 + x, (x * zc + i) * 4 + y))
    return lax.ppermute(mine, ("pool", "head"), perm)


def solution(mesh):
    in_specs = (
        P("pool", "head"),
        P("pool", None, "head"),
        P("pool", None, "head"),
        P("pool", None),
        P(),
        P("head", "pool"),
    )
    return jax.shard_map(body, mesh=mesh, in_specs=in_specs, out_specs=P("pool", "head"), check_vma=False)
```

```python
import functools
import math

import jax
import jax.numpy as jnp
from jax import lax
from jax.experimental import pallas as pl
from jax.experimental.pallas import tpu as pltpu
from jax.sharding import PartitionSpec as P

NX, NY, NZ, NC = 4, 4, 8, 2
HR = 16
HD = 128
MESH = pl.DeviceIdType.MESH
OFFS = (0, NZ - 1, 1, NZ - 2, 2, NZ - 3, 3, 4)


def coords():
    p = lax.axis_index("pool")
    return p // (NZ * NC), (p // NC) % NZ, p % NC


def pid(y, z, c):
    return ((y % NY) * NZ + z % NZ) * NC + c


def gather_kernel(q_ref, w_ref, qs_ref, ws_ref, last_ref, own_sem, z_s, z_r, y_s, y_r, f_s, f_r, c_s, c_r, w_s, w_r, v_s, v_r):
    y, z, c = coords()
    zup, zdn = pid(y, z + 1, c), pid(y, z + NZ - 1, c)
    yu, yd = (y + 1) % NY, (y + NY - 1) % NY
    yup, ydn = pid(yu, z, c), pid(yd, z, c)
    sib = pid(y, z, 1 - c)
    barrier = pltpu.get_barrier_semaphore()
    for peer in (zup, zdn, yup, ydn, sib):
        pl.semaphore_signal(barrier, inc=1, device_id={"pool": peer}, device_id_type=MESH)
    pl.semaphore_wait(barrier, 5)
    sends = []

    def send(src, dst, ss, rs, to):
        d = pltpu.make_async_remote_copy(src_ref=src, dst_ref=dst, send_sem=ss, recv_sem=rs, device_id={"pool": to}, device_id_type=MESH)
        d.start()
        sends.append(d)

    def arrived(dst, ss, rs):
        pltpu.make_async_remote_copy(src_ref=dst, dst_ref=dst, send_sem=ss, recv_sem=rs, device_id={"pool": sib}, device_id_type=MESH).wait_recv()

    rows, wide = q_ref.shape[0], w_ref.shape[0]
    own_q = pltpu.make_async_copy(q_ref, qs_ref.at[c, y, z], own_sem.at[0])
    own_w = pltpu.make_async_copy(w_ref, ws_ref.at[z, c], own_sem.at[1])
    own_q.start()
    own_w.start()
    lo, hi = pl.ds(0, rows // 2), pl.ds(rows // 2, rows - rows // 2)
    wcut = wide // 32 * 16
    wlo, whi = pl.ds(0, wcut), pl.ds(wcut, wide - wcut)

    def q_z(k):
        iu, idn = (z + NZ - (k - 1)) % NZ, (z + k - 1) % NZ
        up = q_ref if k == 1 else qs_ref.at[c, y, iu]
        dn = q_ref if k == 1 else qs_ref.at[c, y, idn]
        if k < 4:
            send(up, qs_ref.at[c, y, iu], z_s.at[2 * k - 2], z_r.at[2 * k - 2], zup)
            send(dn, qs_ref.at[c, y, idn], z_s.at[2 * k - 1], z_r.at[2 * k - 1], zdn)
        else:
            send(up.at[lo], qs_ref.at[c, y, iu, lo], z_s.at[6], z_r.at[6], zup)
            send(dn.at[hi], qs_ref.at[c, y, idn, hi], z_s.at[7], z_r.at[7], zdn)

    def q_z_wait(k):
        iu, idn = (z + NZ - k) % NZ, (z + k) % NZ
        if k < 4:
            arrived(qs_ref.at[c, y, iu], z_s.at[2 * k - 2], z_r.at[2 * k - 2])
            arrived(qs_ref.at[c, y, idn], z_s.at[2 * k - 1], z_r.at[2 * k - 1])
        else:
            arrived(qs_ref.at[c, y, iu, lo], z_s.at[6], z_r.at[6])
            arrived(qs_ref.at[c, y, idn, hi], z_s.at[7], z_r.at[7])

    def w_z(k):
        iu, idn = (z + NZ - (k - 1)) % NZ, (z + k - 1) % NZ
        up = w_ref if k == 1 else ws_ref.at[iu, c]
        dn = w_ref if k == 1 else ws_ref.at[idn, c]
        if k < 4:
            send(up, ws_ref.at[iu, c], w_s.at[2 * k - 2], w_r.at[2 * k - 2], zup)
            send(dn, ws_ref.at[idn, c], w_s.at[2 * k - 1], w_r.at[2 * k - 1], zdn)
        else:
            send(up.at[wlo], ws_ref.at[iu, c, wlo], w_s.at[6], w_r.at[6], zup)
            send(dn.at[whi], ws_ref.at[idn, c, whi], w_s.at[7], w_r.at[7], zdn)

    def w_z_wait(k):
        iu, idn = (z + NZ - k) % NZ, (z + k) % NZ
        if k < 4:
            arrived(ws_ref.at[iu, c], w_s.at[2 * k - 2], w_r.at[2 * k - 2])
            arrived(ws_ref.at[idn, c], w_s.at[2 * k - 1], w_r.at[2 * k - 1])
        else:
            arrived(ws_ref.at[iu, c, wlo], w_s.at[6], w_r.at[6])
            arrived(ws_ref.at[idn, c, whi], w_s.at[7], w_r.at[7])

    def w_core(i):
        zz = (z + OFFS[i]) % NZ
        src = w_ref if i == 0 else ws_ref.at[zz, c]
        send(src, ws_ref.at[zz, c], v_s.at[i], v_r.at[i], sib)

    def q_core(j, i):
        yy, zz = (y + j) % NY, (z + OFFS[i]) % NZ
        src = q_ref if i == 0 and j == 0 else qs_ref.at[c, yy, zz]
        send(src, qs_ref.at[c, yy, zz], c_s.at[8 * j + i], c_r.at[8 * j + i], sib)

    def q_y(i):
        zz = (z + OFFS[i]) % NZ
        src = q_ref if i == 0 else qs_ref.at[c, y, zz]
        send(src, qs_ref.at[c, y, zz], y_s.at[2 * i], y_r.at[2 * i], yup)
        send(src, qs_ref.at[c, y, zz], y_s.at[2 * i + 1], y_r.at[2 * i + 1], ydn)
        q_core(0, i)

    def q_f(i):
        zz = (z + OFFS[i]) % NZ
        arrived(qs_ref.at[c, yd, zz], y_s.at[2 * i], y_r.at[2 * i])
        send(qs_ref.at[c, yd, zz, lo], qs_ref.at[c, yd, zz, lo], f_s.at[2 * i], f_r.at[2 * i], yup)
        arrived(qs_ref.at[c, yu, zz], y_s.at[2 * i + 1], y_r.at[2 * i + 1])
        send(qs_ref.at[c, yu, zz, hi], qs_ref.at[c, yu, zz, hi], f_s.at[2 * i + 1], f_r.at[2 * i + 1], ydn)
        q_core(1, i)
        q_core(3, i)

    def q_f_wait(i):
        zz, yo = (z + OFFS[i]) % NZ, (y + 2) % NY
        arrived(qs_ref.at[c, yo, zz, lo], f_s.at[2 * i], f_r.at[2 * i])
        arrived(qs_ref.at[c, yo, zz, hi], f_s.at[2 * i + 1], f_r.at[2 * i + 1])
        q_core(2, i)

    q_z(1)
    q_y(0)
    w_z(1)
    w_core(0)
    q_z_wait(1)
    q_z(2)
    q_y(1)
    q_y(2)
    q_f(0)
    q_z_wait(2)
    q_z(3)
    q_y(3)
    q_y(4)
    q_f(1)
    q_f(2)
    q_z_wait(3)
    q_z(4)
    q_y(5)
    q_y(6)
    w_z_wait(1)
    w_z(2)
    w_core(1)
    w_core(2)
    q_z_wait(4)
    q_y(7)
    q_f(3)
    q_f(4)
    w_z_wait(2)
    w_z(3)
    w_core(3)
    w_core(4)
    q_f(5)
    q_f(6)
    w_z_wait(3)
    w_z(4)
    w_core(5)
    w_core(6)
    q_f(7)
    for i in range(8):
        q_f_wait(i)
    w_z_wait(4)
    w_core(7)
    own_q.wait()
    own_w.wait()
    for i in range(8):
        zz = (z + OFFS[i]) % NZ
        arrived(ws_ref.at[zz, 1 - c], v_s.at[i], v_r.at[i])
        for j in range(4):
            arrived(qs_ref.at[1 - c, (y + j) % NY, zz], c_s.at[8 * j + i], c_r.at[8 * j + i])
    last = pltpu.make_async_copy(qs_ref.at[:, :, :, rows - 1], last_ref, own_sem.at[0])
    last.start()
    for d in sends:
        d.wait_send()
    last.wait()


def gather(q, wt):
    dma = pltpu.SemaphoreType.DMA
    anyspec = pl.BlockSpec(memory_space=pl.ANY)
    return pl.pallas_call(
        gather_kernel,
        out_shape=(
            pltpu.VMEM((NC, NY, NZ) + q.shape, q.dtype),
            pltpu.VMEM((NZ, NC) + wt.shape, wt.dtype),
            pltpu.VMEM((NC, NY, NZ) + q.shape[1:], q.dtype),
        ),
        in_specs=[anyspec] * 2,
        out_specs=(anyspec,) * 3,
        scratch_shapes=[dma((n,)) for n in (2, 8, 8, 16, 16, 16, 16, 32, 32, 8, 8, 8, 8)],
        compiler_params=pltpu.CompilerParams(collective_id=0, has_side_effects=True, vmem_limit_bytes=2**20),
        name="gather",
    )(q, wt)


NEG = -1e30
CHUNK = 32
BATCH = 8
ROWS = 2048
GROUPS = 24


def with_ids(queries, span_ids):
    flat = span_ids.T
    picks, rows = flat.shape
    tile = jnp.concatenate([flat // 32, flat % 32, jnp.zeros((picks, 128 - 2 * rows), jnp.int32)], axis=1)
    return jnp.concatenate([queries, tile.astype(queries.dtype)[None]], axis=0)


def list_requests(last_ref, slot_ref, first_ref, second_ref, lists_ref, counts_ref):
    spans = lists_ref.shape[0]
    me = lax.axis_index("pool")
    slots = slot_ref[...]
    where_id = lax.broadcasted_iota(jnp.int32, slots.shape, 0) * 128 + lax.broadcasted_iota(jnp.int32, slots.shape, 1)
    names = []
    for s in range(spans):
        found = jnp.where(slots == me * spans + s, where_id, 0).astype(jnp.float32)
        found = jnp.sum(found, axis=0, keepdims=True)
        names.append(jnp.broadcast_to(jnp.sum(found, axis=1, keepdims=True), (16, 128)))
    lane = lax.broadcasted_iota(jnp.int32, (8, 128), 1)
    sub = lax.broadcasted_iota(jnp.int32, (8, 128), 0)
    none = 1000

    def block(b, _):
        t = last_ref[b].astype(jnp.float32)
        ids = t * 32.0 + pltpu.roll(t, 96, 1)
        named = jnp.zeros((8, 128), jnp.float32)
        for s in range(spans):
            hit = jnp.where(ids == names[s], 1.0, 0.0)
            hit = jnp.max(hit, axis=0, keepdims=True)
            named = jnp.where(sub == s, jnp.broadcast_to(hit, (8, 128)), named)
        hit = (named > 0.0) & (lane < 32)
        low = jnp.min(jnp.where(hit, lane, none).astype(jnp.float32), axis=1, keepdims=True)
        high = jnp.max(jnp.where(hit, lane, -1).astype(jnp.float32), axis=1, keepdims=True)
        at = pl.ds(pl.multiple_of(b * 8, 8), 8)
        first_ref[at] = jnp.broadcast_to(low, (8, 128))
        second_ref[at] = jnp.broadcast_to(jnp.where(high > low, high, float(none)), (8, 128))
        return 0

    blocks = last_ref.shape[0]
    lax.fori_loop(0, blocks, block, 0, unroll=4)
    b = lax.broadcasted_iota(jnp.int32, (blocks, 128), 0)
    k = lax.broadcasted_iota(jnp.int32, (blocks, 128), 1).astype(jnp.float32)
    z, y, c = b % NZ, b // NZ % NY, b // (NZ * NY)
    early = c * 512 + (z * NY + y) * HR
    late = ROWS // 2 + c * 512 + (y * NZ + z) * HR - HR
    below = jnp.where(lax.broadcasted_iota(jnp.int32, (blocks, blocks), 0) > lax.broadcasted_iota(jnp.int32, (blocks, blocks), 1), 1.0, 0.0).astype(jnp.bfloat16)
    for s in range(spans):
        count = jnp.zeros((1, 128), jnp.float32)
        listing = jnp.zeros((1, 128), jnp.int32)
        for ref in (first_ref, second_ref):
            row = ref[pl.ds(s, blocks, stride=8), :]
            used = row < 32.0
            one = jnp.where(used, 1.0, 0.0)
            rank = jnp.dot(below, one.astype(jnp.bfloat16), preferred_element_type=jnp.float32) + count
            r = row.astype(jnp.int32)
            place = jnp.where(r < HR, early, late) + r + 4096 * (b * 33 + r)
            listing += jnp.sum(jnp.where(used & (rank == k), place, 0), axis=0, keepdims=True)
            count += jnp.sum(one, axis=0, keepdims=True)
        lists_ref[s:s + 1, :] = jnp.where(lane[0:1].astype(jnp.float32) < count, listing, ROWS)
        counts_ref[s:s + 1, :] = count.astype(jnp.int32)


def attend_kernel(last_ref, slot_ref, q_ref, k_hbm, v_hbm, d_ref, st_ref, first_ref, second_ref, lists_ref, counts_ref, list_ref, count_ref, lsem, kbuf, vbuf, l0, l1, p0, p1, e0, e1, ksem, vsem):
    spans = kbuf.shape[0]
    for s in range(spans):
        for hbm, buf, sem in ((k_hbm, kbuf, ksem), (v_hbm, vbuf, vsem)):
            d = pltpu.make_async_copy(hbm.at[s], buf.at[s], sem.at[s])
            d.start()

    list_requests(last_ref, slot_ref, first_ref, second_ref, lists_ref, counts_ref)
    moves = [pltpu.make_async_copy(lists_ref, list_ref, lsem.at[0]), pltpu.make_async_copy(counts_ref, count_ref, lsem.at[1])]
    for d in moves:
        d.start()

    def clear(i, _):
        d_ref[pl.ds(i * 8, 8)] = jnp.zeros((8, 16, 128), jnp.bfloat16)
        return 0

    lax.fori_loop(0, ROWS // 8 + 1, clear, 0)
    st_ref[...] = jnp.full(st_ref.shape, NEG, jnp.float32)
    for d in moves:
        d.wait()
    scale2 = math.log2(math.e) / math.sqrt(HD)
    lane = lax.broadcasted_iota(jnp.int32, (16, 128), 1)

    def span(s, _):
        pltpu.make_async_copy(k_hbm.at[s], kbuf.at[s], ksem.at[s]).wait()
        pltpu.make_async_copy(v_hbm.at[s], vbuf.at[s], vsem.at[s]).wait()
        n = count_ref[s, 0]

        def chunk(j, _):
            base = j * CHUNK
            for i in range(0, CHUNK, 2):
                a = q_ref[list_ref[s, base + i] >> 12].astype(jnp.float32)
                b = q_ref[list_ref[s, base + i + 1] >> 12].astype(jnp.float32)
                l0[pl.ds(i * 8, 16)] = jnp.concatenate([a[0:8], b[0:8]], axis=0).astype(jnp.bfloat16)
                l1[pl.ds(i * 8, 16)] = jnp.concatenate([a[8:16], b[8:16]], axis=0).astype(jnp.bfloat16)
            for kv, (l, p, e) in enumerate(((l0, p0, e0), (l1, p1, e1))):
                keys = kbuf[s, :, kv * HD:(kv + 1) * HD]
                vals = vbuf[s, :, kv * HD:(kv + 1) * HD]
                sc = lax.dot_general(l[...], keys, (((1,), (1,)), ((), ())), preferred_element_type=jnp.float32) * scale2
                m = jnp.max(sc, axis=1, keepdims=True)
                ex = jnp.exp2(sc - m)
                tot = jnp.sum(ex, axis=1, keepdims=True)
                pv = jnp.dot(ex.astype(jnp.bfloat16), vals, preferred_element_type=jnp.float32)
                p[...] = pv / tot
                e[...] = jnp.broadcast_to(m + jnp.log2(tot), e.shape)
            for first in range(0, CHUNK, BATCH):
                done = []
                for i in range(first, first + BATCH):
                    place = list_ref[s, base + i] & 4095
                    early = place < ROWS // 2
                    g = jnp.where(early, place >> 6, 8 + (place >> 7))
                    at = place & jnp.where(early, 63, 127)
                    here = lane == at
                    new = jnp.concatenate([p0[pl.ds(i * 8, 8)], p1[pl.ds(i * 8, 8)]], axis=0)
                    le = jnp.concatenate([e0[pl.ds(i * 8, 8)], e1[pl.ds(i * 8, 8)]], axis=0)
                    old = d_ref[place].astype(jnp.float32)
                    ol = jnp.max(jnp.where(here, st_ref[g], -3e38), axis=1, keepdims=True)
                    ex = jnp.exp2(-jnp.abs(le - ol))
                    both = 1.0 + ex
                    w = jnp.where(le > ol, 1.0, ex) / both
                    done.append((place, g, here, old + w * (new - old), jnp.maximum(le, ol) + jnp.log2(both)))
                for place, g, here, tile, le in done:
                    d_ref[place] = tile.astype(jnp.bfloat16)
                for place, g, here, tile, le in done:
                    st_ref[g] = jnp.where(here, le, st_ref[g])
            return 0

        lax.fori_loop(0, (n + CHUNK - 1) // CHUNK, chunk, 0)
        return 0

    lax.fori_loop(0, spans, span, 0)


def attend(last, span_slot, qs, span_keys, span_values):
    anyspec = pl.BlockSpec(memory_space=pl.ANY)
    vmem = pl.BlockSpec(memory_space=pltpu.VMEM)
    rows = CHUNK * 8
    spans = span_keys.shape[0]
    blocks = NC * NY * NZ
    return pl.pallas_call(
        attend_kernel,
        out_shape=(pltpu.VMEM((ROWS + 8, 16, HD), jnp.bfloat16), pltpu.VMEM((GROUPS + 1, 16, 128), jnp.float32)),
        in_specs=[vmem, vmem, vmem, anyspec, anyspec],
        out_specs=(vmem, vmem),
        scratch_shapes=[pltpu.VMEM((blocks * 8, 128), jnp.float32)] * 2
        + [pltpu.VMEM((spans, 128), jnp.int32)] * 2
        + [pltpu.SMEM((spans, 128), jnp.int32)] * 2
        + [pltpu.SemaphoreType.DMA((2,))]
        + [pltpu.VMEM(span_keys.shape, jnp.bfloat16)] * 2
        + [pltpu.VMEM((rows, HD), jnp.bfloat16)] * 2
        + [pltpu.VMEM((rows, HD), jnp.float32)] * 4
        + [pltpu.SemaphoreType.DMA((spans,))] * 2,
        compiler_params=pltpu.CompilerParams(vmem_limit_bytes=24 * 2**20),
        name="attend",
    )(
        last.reshape(blocks, 16, 128),
        span_slot.reshape(-1, 128),
        pltpu.with_memory_space_constraint(qs.reshape(-1, 16, HD), pltpu.VMEM),
        pltpu.with_memory_space_constraint(span_keys, pltpu.HBM),
        pltpu.with_memory_space_constraint(span_values, pltpu.HBM),
    )


def merge_kernel(d_ref, st_ref, w_ref, out_ref,
                 ma, mb, ra, rb, sa, sb, rsa, rsb,
                 ua, da, usa, dsa, ub, db, usb, dsb, ya, ysa, uz, dz, usz, dsz,
                 fa, near, terms, xin, tsum, fin,
                 n_s, n_r, t_s, t_r, g_s, g_r,
                 own_sem, sib_s, sib_r, ua_s, ua_r, da_s, da_r, usa_s, usa_r, dsa_s, dsa_r,
                 ub_s, ub_r, db_s, db_r, usb_s, usb_r, dsb_s, dsb_r,
                 ya_s, ya_r, ysa_s, ysa_r, uz_s, uz_r, dz_s, dz_r, usz_s, usz_r, dsz_s, dsz_r):
    y, z, c = coords()
    zup, zdn = pid(y, z + 1, c), pid(y, z + NZ - 1, c)
    yup, ydn = pid(y + 1, z, c), pid(y + NY - 1, z, c)
    sib = pid(y, z, 1 - c)
    lane = lax.broadcasted_iota(jnp.int32, (16, 128), 1)

    x = lax.axis_index("head")

    def d_a(core, w):
        return d_ref.at[pl.ds(core * 512 + w * (NY * HR), NY * HR)]

    def d_b(core, w):
        return d_ref.at[pl.ds(ROWS // 2 + core * 512 + w * (NZ * HR), NZ * HR)]

    loads = [
        pltpu.make_async_copy(st_ref.at[pl.ds(c * NZ, NZ)], sa, own_sem.at[0]),
        pltpu.make_async_copy(st_ref.at[pl.ds(2 * NZ + c * NY, NY)], sb, own_sem.at[1]),
    ]
    for d in loads:
        d.start()
    barrier = pltpu.get_barrier_semaphore()
    for peer in (pid(y + 1, z, c), pid(y + 2, z, c), pid(y + 3, z, c), zup, zdn, sib):
        pl.semaphore_signal(barrier, inc=1, device_id={"pool": peer, "head": x}, device_id_type=MESH)
    me = pid(y, z, c)
    for d in (1, 2, 3):
        pl.semaphore_signal(barrier, inc=1, device_id={"pool": me, "head": (x + d) % NX}, device_id_type=MESH)
    flip = {"pool": pid(x, z, c), "head": y}

    @pl.when(x != y)
    def _():
        pl.semaphore_signal(barrier, inc=1, device_id=flip, device_id_type=MESH)
        pl.semaphore_wait(barrier, 10)

    @pl.when(x == y)
    def _():
        pl.semaphore_wait(barrier, 9)

    sends = []

    def send(src, dst, ss, rs, to, head=x):
        d = pltpu.make_async_remote_copy(src_ref=src, dst_ref=dst, send_sem=ss, recv_sem=rs, device_id={"pool": to, "head": head}, device_id_type=MESH)
        d.start()
        sends.append(d)

    def arrived(dst, ss, rs):
        pltpu.make_async_remote_copy(src_ref=dst, dst_ref=dst, send_sem=ss, recv_sem=rs, device_id={"pool": sib}, device_id_type=MESH).wait_recv()

    def zz(d):
        return (z + d + NZ) % NZ

    def yy(d):
        return (y + d + NY) % NY

    a_order = [4, 3, -3, 2, -2, 1, -1, 0]
    b_order = [2, 1, -1, 0]
    send(st_ref.at[pl.ds((1 - c) * NZ, NZ)], rsa, sib_s.at[12], sib_r.at[12], sib)
    send(st_ref.at[pl.ds(2 * NZ + (1 - c) * NY, NY)], rsb, sib_s.at[13], sib_r.at[13], sib)

    def sib_a(i):
        w = zz(a_order[i])
        send(d_a(1 - c, w), ra.at[w], sib_s.at[i], sib_r.at[i], sib)

    def sib_b(i):
        w = yy(b_order[i])
        send(d_b(1 - c, w), rb.at[w], sib_s.at[8 + i], sib_r.at[8 + i], sib)

    sib_a(0)
    sib_b(0)
    sib_a(1)
    sib_a(2)
    sib_b(1)
    sib_b(2)
    sib_a(3)
    sib_a(4)
    sib_a(5)
    sib_a(6)
    sib_b(3)
    sib_a(7)

    def blend(dst, src, wt, rows=HR, start=0, base=None):
        base = dst if base is None else base
        for i in range(start, start + rows):
            w = jnp.broadcast_to(wt[:, i:i + 1], (16, 128))
            a = base[i].astype(jnp.float32)
            b = src[i].astype(jnp.float32)
            dst[i] = (a + w * (b - a)).astype(jnp.bfloat16)

    def join(own, other):
        top = jnp.maximum(own, other)
        low = jnp.minimum(own, other)
        new = top + jnp.log2(1.0 + jnp.exp2(low - top))
        return new, jnp.exp2(other - new)

    def turned(wt, by):
        return pltpu.roll(wt, (128 - by) % 128, 1)

    for d in loads:
        d.wait()
    arrived(rsa, sib_s.at[12], sib_r.at[12])
    arrived(rsb, sib_s.at[13], sib_r.at[13])

    def core_a(i):
        w = zz(a_order[i])
        arrived(ra.at[w], sib_s.at[i], sib_r.at[i])
        new, wt = join(sa[w], rsa[w])
        sa[w] = new

        def cell(j, wt):
            part = pl.ds(j * HR, HR)
            blend(ma.at[w, j], ra.at[w, part], wt, base=d_a(c, w).at[part])
            return pltpu.roll(wt, 128 - HR, 1)

        lax.fori_loop(0, NY, cell, wt)

    def core_b(i):
        w = yy(b_order[i])
        arrived(rb.at[w], sib_s.at[8 + i], sib_r.at[8 + i])
        new, wt = join(sb[w], rsb[w])
        sb[w] = new

        def cell(j, wt):
            part = pl.ds(j * HR, HR)
            blend(mb.at[w, j], rb.at[w, part], wt, base=d_b(c, w).at[part])
            return pltpu.roll(wt, 128 - HR, 1)

        lax.fori_loop(0, NZ, cell, wt)

    def a_first():
        w = zz(4)
        st = sa[w]
        usa[4] = jnp.where(lane < 2 * HR, st, NEG)
        dsa[4] = jnp.where(lane < 2 * HR, NEG, st)
        send(usa.at[4], usa.at[0], usa_s.at[0], usa_r.at[0], zup)
        send(dsa.at[4], dsa.at[0], dsa_s.at[0], dsa_r.at[0], zdn)
        for j in (0, 1):
            send(ma.at[w, j], ua.at[0, j], ua_s.at[j], ua_r.at[j], zup)
            send(ma.at[w, 2 + j], da.at[0, 2 + j], da_s.at[2 + j], da_r.at[2 + j], zdn)

    def a_step(k):
        wu, wd = zz(4 - k), zz(k - 4)
        arrived(usa.at[k - 1], usa_s.at[k - 1], usa_r.at[k - 1])
        newu, wtu = join(sa[wu], usa[k - 1])
        sa[wu] = newu
        if k < 4:
            send(sa.at[wu], usa.at[k], usa_s.at[k], usa_r.at[k], zup)
        arrived(dsa.at[k - 1], dsa_s.at[k - 1], dsa_r.at[k - 1])
        newd, wtd = join(sa[wd], dsa[k - 1])
        sa[wd] = newd
        if k < 4:
            send(sa.at[wd], dsa.at[k], dsa_s.at[k], dsa_r.at[k], zdn)

        for j in range(NY):
            n = 4 * (k - 1) + j
            if k > 1 or j < 2:
                arrived(ua.at[k - 1, j], ua_s.at[n], ua_r.at[n])
                blend(ma.at[wu, j], ua.at[k - 1, j], turned(wtu, HR * j))
            if k < 4:
                send(ma.at[wu, j], ua.at[k, j], ua_s.at[n + 4], ua_r.at[n + 4], zup)
            if k > 1 or j >= 2:
                arrived(da.at[k - 1, j], da_s.at[n], da_r.at[n])
                blend(ma.at[wd, j], da.at[k - 1, j], turned(wtd, HR * j))
            if k < 4:
                send(ma.at[wd, j], da.at[k, j], da_s.at[n + 4], da_r.at[n + 4], zdn)

    def b_first():
        w = yy(2)
        st = sb[w]
        usb[2] = jnp.where(lane < 4 * HR, st, NEG)
        dsb[2] = jnp.where(lane < 4 * HR, NEG, st)
        send(usb.at[2], usb.at[0], usb_s.at[0], usb_r.at[0], yup)
        send(dsb.at[2], dsb.at[0], dsb_s.at[0], dsb_r.at[0], ydn)
        for j in range(4):
            send(mb.at[w, j], ub.at[0, j], ub_s.at[j], ub_r.at[j], yup)
            send(mb.at[w, 4 + j], db.at[0, 4 + j], db_s.at[4 + j], db_r.at[4 + j], ydn)

    def b_step(k):
        wu, wd = yy(2 - k), yy(k - 2)
        arrived(usb.at[k - 1], usb_s.at[k - 1], usb_r.at[k - 1])
        newu, wtu = join(sb[wu], usb[k - 1])
        sb[wu] = newu
        if k < 2:
            send(sb.at[wu], usb.at[k], usb_s.at[k], usb_r.at[k], yup)
        arrived(dsb.at[k - 1], dsb_s.at[k - 1], dsb_r.at[k - 1])
        newd, wtd = join(sb[wd], dsb[k - 1])
        sb[wd] = newd
        if k < 2:
            send(sb.at[wd], dsb.at[k], dsb_s.at[k], dsb_r.at[k], ydn)
        for j in range(NZ):
            n = 8 * (k - 1) + j
            if k > 1 or j < 4:
                arrived(ub.at[k - 1, j], ub_s.at[n], ub_r.at[n])
                blend(mb.at[wu, j], ub.at[k - 1, j], turned(wtu, HR * j))
            if k < 2:
                send(mb.at[wu, j], ub.at[k, j], ub_s.at[n + 8], ub_r.at[n + 8], yup)
            if k > 1 or j >= 4:
                arrived(db.at[k - 1, j], db_s.at[n], db_r.at[n])
                blend(mb.at[wd, j], db.at[k - 1, j], turned(wtd, HR * j))
            if k < 2:
                send(mb.at[wd, j], db.at[k, j], db_s.at[n + 8], db_r.at[n + 8], ydn)

    def a_y():
        for d in (1, 2, 3):
            w = yy(d)
            send(sa.at[z], ysa.at[d - 1], ysa_s.at[d - 1], ysa_r.at[d - 1], pid(y + d, z, c))
            send(ma.at[z, w], ya.at[d - 1], ya_s.at[d - 1], ya_r.at[d - 1], pid(y + d, z, c))

    def a_y_end():
        total = turned(sa[z], HR * y)
        for d in (1, 3, 2):
            arrived(ysa.at[d - 1], ysa_s.at[d - 1], ysa_r.at[d - 1])
            total, wt = join(total, turned(ysa[d - 1], HR * y))
            arrived(ya.at[d - 1], ya_s.at[d - 1], ya_r.at[d - 1])
            blend(ma.at[z, y], ya.at[d - 1], wt)

    def bz_first():
        w = zz(4)
        usz[4] = turned(sb[y], HR * w)
        send(usz.at[4], usz.at[0], usz_s.at[0], usz_r.at[0], zup)
        send(usz.at[4], dsz.at[0], dsz_s.at[0], dsz_r.at[0], zdn)
        lo, hi = pl.ds(0, HR // 2), pl.ds(HR // 2, HR // 2)
        send(mb.at[y, w, lo], uz.at[0, lo], uz_s.at[0], uz_r.at[0], zup)
        send(mb.at[y, w, hi], dz.at[0, hi], dz_s.at[0], dz_r.at[0], zdn)

    def bz_step(k):
        wu, wd = zz(4 - k), zz(k - 4)
        lo, hi = pl.ds(0, HR // 2), pl.ds(HR // 2, HR // 2)
        arrived(usz.at[k - 1], usz_s.at[k - 1], usz_r.at[k - 1])
        ru = usz[k - 1]
        if k == 1:
            ru = jnp.where(lane < HR // 2, ru, NEG)
        newu, wtu = join(turned(sb[y], HR * wu), ru)
        if k < 4:
            usz[4 + k] = newu
            send(usz.at[4 + k], usz.at[k], usz_s.at[k], usz_r.at[k], zup)
        arrived(dsz.at[k - 1], dsz_s.at[k - 1], dsz_r.at[k - 1])
        rd = dsz[k - 1]
        if k == 1:
            rd = jnp.where(lane < HR // 2, NEG, rd)
        own = turned(sb[y], HR * wd) if k < 4 else newu
        newd, wtd = join(own, rd)
        if k < 4:
            dsz[4 + k] = newd
            send(dsz.at[4 + k], dsz.at[k], dsz_s.at[k], dsz_r.at[k], zdn)
        if k == 1:
            arrived(uz.at[0, lo], uz_s.at[0], uz_r.at[0])
            blend(mb.at[y, wu], uz.at[0], wtu, HR // 2, 0)
        else:
            arrived(uz.at[k - 1], uz_s.at[k - 1], uz_r.at[k - 1])
            blend(mb.at[y, wu], uz.at[k - 1], wtu)
        if k < 4:
            send(mb.at[y, wu], uz.at[k], uz_s.at[k], uz_r.at[k], zup)
        if k == 1:
            arrived(dz.at[0, hi], dz_s.at[0], dz_r.at[0])
            blend(mb.at[y, wd], dz.at[0], wtd, HR // 2, HR // 2)
        else:
            arrived(dz.at[k - 1], dz_s.at[k - 1], dz_r.at[k - 1])
            blend(mb.at[y, wd], dz.at[k - 1], wtd)
        if k < 4:
            send(mb.at[y, wd], dz.at[k], dz_s.at[k], dz_r.at[k], zdn)

    def share(h, cell):
        fa[...] = cell[...].astype(jnp.float32).reshape(HR * 16, HD)
        for i in range(16):
            near[h, y, :, i * HD:(i + 1) * HD] = fa[pl.ds(i, HR, stride=16), :].astype(jnp.bfloat16)
        for d in (1, 2, 3):
            n = 3 * h + d - 1
            send(near.at[h, y], near.at[h, y], n_s.at[n], n_r.at[n], pid(y + d, z, c))

    def project(h):
        for d in (1, 3, 2):
            n = 3 * h + d - 1
            arrived(near.at[h, yy(-d)], n_s.at[n], n_r.at[n])
        rows = near[h].reshape(NY * HR, near.shape[-1])
        wide = w_ref.shape[0]
        for lo in range(0, wide, 256):
            t = lax.dot_general(rows, w_ref[lo:lo + 256, :], (((1,), (1,)), ((), ())), preferred_element_type=jnp.float32)
            terms[h, :, :, lo:lo + 256] = t.astype(jnp.bfloat16).reshape(NY, HR, 256)
        for d in (1, 2, 3):
            n = 3 * h + d - 1
            to = (x + d) % NX
            send(terms.at[h, to], xin.at[h, d - 1], t_s.at[n], t_r.at[n], me, to)

    def finish(h):
        total = terms[h, x].astype(jnp.float32)
        for d in (1, 3, 2):
            n = 3 * h + d - 1
            arrived(xin.at[h, d - 1], t_s.at[n], t_r.at[n])
            total += xin[h, d - 1].astype(jnp.float32)
        tsum[h] = total.astype(jnp.bfloat16)

        @pl.when(x != y)
        def _():
            pltpu.make_async_remote_copy(src_ref=tsum.at[h], dst_ref=fin.at[h], send_sem=g_s.at[h], recv_sem=g_r.at[h], device_id=flip, device_id_type=MESH).start()

    def land(h):
        @pl.when(x != y)
        def _():
            pltpu.make_async_remote_copy(src_ref=tsum.at[h], dst_ref=fin.at[h], send_sem=g_s.at[h], recv_sem=g_r.at[h], device_id=flip, device_id_type=MESH).wait()
            out_ref[pl.ds(h * HR, HR)] = fin[h]

        @pl.when(x == y)
        def _():
            out_ref[pl.ds(h * HR, HR)] = tsum[h]

    core_a(0)
    a_first()
    core_b(0)
    b_first()
    core_a(1)
    core_a(2)
    a_step(1)
    core_b(1)
    core_b(2)
    b_step(1)
    core_a(3)
    core_a(4)
    a_step(2)
    core_a(5)
    core_a(6)
    a_step(3)
    core_b(3)
    b_step(2)
    bz_first()
    core_a(7)
    a_step(4)
    a_y()
    bz_step(1)
    bz_step(2)
    a_y_end()
    share(0, ma.at[z, y])
    bz_step(3)
    bz_step(4)
    share(1, mb.at[y, z])
    project(0)
    project(1)
    finish(0)
    finish(1)
    land(0)
    land(1)
    for d in sends:
        d.wait_send()


def merge(d, st, weight):
    dma = pltpu.SemaphoreType.DMA
    bf, f32 = jnp.bfloat16, jnp.float32

    def v(*shape, dtype=bf):
        return pltpu.VMEM(shape + (16, 128), dtype)

    anyspec = pl.BlockSpec(memory_space=pl.ANY)
    vmem = pl.BlockSpec(memory_space=pltpu.VMEM)
    sems = [6, 6, 6, 6, 2, 2]
    sems += [2, 14, 14, 16, 16, 16, 16, 4, 4, 4, 4, 16, 16, 16, 16, 2, 2, 2, 2, 3, 3, 3, 3, 4, 4, 4, 4, 4, 4, 4, 4]
    wide, deep = weight.shape
    return pl.pallas_call(
        merge_kernel,
        out_shape=jax.ShapeDtypeStruct((2 * HR, wide), bf),
        in_specs=[vmem, vmem, vmem],
        out_specs=vmem,
        scratch_shapes=[
            v(NZ, NY, HR), v(NY, NZ, HR), v(NZ, NY * HR), v(NY, NZ * HR),
            v(NZ, dtype=f32), v(NY, dtype=f32), v(NZ, dtype=f32), v(NY, dtype=f32),
            v(4, NY, HR), v(4, NY, HR), v(5, dtype=f32), v(5, dtype=f32),
            v(2, NZ, HR), v(2, NZ, HR), v(3, dtype=f32), v(3, dtype=f32),
            v(3, HR), v(3, dtype=f32),
            v(4, HR), v(4, HR), v(8, dtype=f32), v(8, dtype=f32),
            pltpu.VMEM((HR * 16, HD), f32),
            pltpu.VMEM((2, NY, HR, deep), bf),
            pltpu.VMEM((2, NY, HR, wide), bf),
            pltpu.VMEM((2, 3, HR, wide), bf),
            pltpu.VMEM((2, HR, wide), bf),
            pltpu.VMEM((2, HR, wide), bf),
        ] + [dma((n,)) for n in sems],
        compiler_params=pltpu.CompilerParams(collective_id=1, has_side_effects=True, vmem_limit_bytes=20 * 2**20),
        name="merge",
    )(d, st, pltpu.with_memory_space_constraint(weight, pltpu.VMEM))


def body(queries, span_keys, span_values, span_ids, span_slot, out_weight):
    rows, width = queries.shape
    qs, ws, last = gather(with_ids(queries.reshape(rows, width // HD, HD), span_ids), out_weight.T)
    d, st = attend(last, span_slot, qs, span_keys, span_values)
    return merge(d, st, ws.reshape(-1, width))


def solution(mesh):
    in_specs = (
        P("pool", "head"),
        P("pool", None, "head"),
        P("pool", None, "head"),
        P("pool", None),
        P(),
        P("head", "pool"),
    )
    return jax.shard_map(body, mesh=mesh, in_specs=in_specs, out_specs=P("pool", "head"), check_vma=False)
```

```python
import functools
import math

import jax
import jax.numpy as jnp
from jax import lax
from jax.experimental import pallas as pl
from jax.experimental.pallas import tpu as pltpu
from jax.sharding import PartitionSpec as P

NX, NY, NZ, NC = 4, 4, 8, 2
HR = 16
HD = 128
MESH = pl.DeviceIdType.MESH
OFFS = (0, NZ - 1, 1, NZ - 2, 2, NZ - 3, 3, 4)


def coords():
    p = lax.axis_index("pool")
    return p // (NZ * NC), (p // NC) % NZ, p % NC


def pid(y, z, c):
    return ((y % NY) * NZ + z % NZ) * NC + c


def gather_kernel(q_ref, w_ref, qs_ref, ws_ref, last_ref, own_sem, z_s, z_r, y_s, y_r, f_s, f_r, c_s, c_r, w_s, w_r, v_s, v_r):
    y, z, c = coords()
    zup, zdn = pid(y, z + 1, c), pid(y, z + NZ - 1, c)
    yu, yd = (y + 1) % NY, (y + NY - 1) % NY
    yup, ydn = pid(yu, z, c), pid(yd, z, c)
    sib = pid(y, z, 1 - c)
    barrier = pltpu.get_barrier_semaphore()
    for peer in (zup, zdn, yup, ydn, sib):
        pl.semaphore_signal(barrier, inc=1, device_id={"pool": peer}, device_id_type=MESH)
    pl.semaphore_wait(barrier, 5)
    sends = []

    def send(src, dst, ss, rs, to):
        d = pltpu.make_async_remote_copy(src_ref=src, dst_ref=dst, send_sem=ss, recv_sem=rs, device_id={"pool": to}, device_id_type=MESH)
        d.start()
        sends.append(d)

    def arrived(dst, ss, rs):
        pltpu.make_async_remote_copy(src_ref=dst, dst_ref=dst, send_sem=ss, recv_sem=rs, device_id={"pool": sib}, device_id_type=MESH).wait_recv()

    rows, wide = q_ref.shape[0], w_ref.shape[0]
    own_q = pltpu.make_async_copy(q_ref, qs_ref.at[c, y, z], own_sem.at[0])
    own_w = pltpu.make_async_copy(w_ref, ws_ref.at[z, c], own_sem.at[1])
    own_q.start()
    own_w.start()
    lo, hi = pl.ds(0, rows // 2), pl.ds(rows // 2, rows - rows // 2)
    wcut = wide // 32 * 16
    wlo, whi = pl.ds(0, wcut), pl.ds(wcut, wide - wcut)

    def q_z(k):
        iu, idn = (z + NZ - (k - 1)) % NZ, (z + k - 1) % NZ
        up = q_ref if k == 1 else qs_ref.at[c, y, iu]
        dn = q_ref if k == 1 else qs_ref.at[c, y, idn]
        if k < 4:
            send(up, qs_ref.at[c, y, iu], z_s.at[2 * k - 2], z_r.at[2 * k - 2], zup)
            send(dn, qs_ref.at[c, y, idn], z_s.at[2 * k - 1], z_r.at[2 * k - 1], zdn)
        else:
            send(up.at[lo], qs_ref.at[c, y, iu, lo], z_s.at[6], z_r.at[6], zup)
            send(dn.at[hi], qs_ref.at[c, y, idn, hi], z_s.at[7], z_r.at[7], zdn)

    def q_z_wait(k):
        iu, idn = (z + NZ - k) % NZ, (z + k) % NZ
        if k < 4:
            arrived(qs_ref.at[c, y, iu], z_s.at[2 * k - 2], z_r.at[2 * k - 2])
            arrived(qs_ref.at[c, y, idn], z_s.at[2 * k - 1], z_r.at[2 * k - 1])
        else:
            arrived(qs_ref.at[c, y, iu, lo], z_s.at[6], z_r.at[6])
            arrived(qs_ref.at[c, y, idn, hi], z_s.at[7], z_r.at[7])

    def w_z(k):
        iu, idn = (z + NZ - (k - 1)) % NZ, (z + k - 1) % NZ
        up = w_ref if k == 1 else ws_ref.at[iu, c]
        dn = w_ref if k == 1 else ws_ref.at[idn, c]
        if k < 4:
            send(up, ws_ref.at[iu, c], w_s.at[2 * k - 2], w_r.at[2 * k - 2], zup)
            send(dn, ws_ref.at[idn, c], w_s.at[2 * k - 1], w_r.at[2 * k - 1], zdn)
        else:
            send(up.at[wlo], ws_ref.at[iu, c, wlo], w_s.at[6], w_r.at[6], zup)
            send(dn.at[whi], ws_ref.at[idn, c, whi], w_s.at[7], w_r.at[7], zdn)

    def w_z_wait(k):
        iu, idn = (z + NZ - k) % NZ, (z + k) % NZ
        if k < 4:
            arrived(ws_ref.at[iu, c], w_s.at[2 * k - 2], w_r.at[2 * k - 2])
            arrived(ws_ref.at[idn, c], w_s.at[2 * k - 1], w_r.at[2 * k - 1])
        else:
            arrived(ws_ref.at[iu, c, wlo], w_s.at[6], w_r.at[6])
            arrived(ws_ref.at[idn, c, whi], w_s.at[7], w_r.at[7])

    def w_core(i):
        zz = (z + OFFS[i]) % NZ
        src = w_ref if i == 0 else ws_ref.at[zz, c]
        send(src, ws_ref.at[zz, c], v_s.at[i], v_r.at[i], sib)

    def q_core(j, i):
        yy, zz = (y + j) % NY, (z + OFFS[i]) % NZ
        src = q_ref if i == 0 and j == 0 else qs_ref.at[c, yy, zz]
        send(src, qs_ref.at[c, yy, zz], c_s.at[8 * j + i], c_r.at[8 * j + i], sib)

    def q_y(i):
        zz = (z + OFFS[i]) % NZ
        src = q_ref if i == 0 else qs_ref.at[c, y, zz]
        send(src, qs_ref.at[c, y, zz], y_s.at[2 * i], y_r.at[2 * i], yup)
        send(src, qs_ref.at[c, y, zz], y_s.at[2 * i + 1], y_r.at[2 * i + 1], ydn)
        q_core(0, i)

    def q_f(i):
        zz = (z + OFFS[i]) % NZ
        arrived(qs_ref.at[c, yd, zz], y_s.at[2 * i], y_r.at[2 * i])
        send(qs_ref.at[c, yd, zz, lo], qs_ref.at[c, yd, zz, lo], f_s.at[2 * i], f_r.at[2 * i], yup)
        arrived(qs_ref.at[c, yu, zz], y_s.at[2 * i + 1], y_r.at[2 * i + 1])
        send(qs_ref.at[c, yu, zz, hi], qs_ref.at[c, yu, zz, hi], f_s.at[2 * i + 1], f_r.at[2 * i + 1], ydn)
        q_core(1, i)
        q_core(3, i)

    def q_f_wait(i):
        zz, yo = (z + OFFS[i]) % NZ, (y + 2) % NY
        arrived(qs_ref.at[c, yo, zz, lo], f_s.at[2 * i], f_r.at[2 * i])
        arrived(qs_ref.at[c, yo, zz, hi], f_s.at[2 * i + 1], f_r.at[2 * i + 1])
        q_core(2, i)

    q_z(1)
    q_y(0)
    w_z(1)
    w_core(0)
    q_z_wait(1)
    q_z(2)
    q_y(1)
    q_y(2)
    q_f(0)
    q_z_wait(2)
    q_z(3)
    q_y(3)
    q_y(4)
    q_f(1)
    q_f(2)
    q_z_wait(3)
    q_z(4)
    q_y(5)
    q_y(6)
    w_z_wait(1)
    w_z(2)
    w_core(1)
    w_core(2)
    q_z_wait(4)
    q_y(7)
    q_f(3)
    q_f(4)
    w_z_wait(2)
    w_z(3)
    w_core(3)
    w_core(4)
    q_f(5)
    q_f(6)
    w_z_wait(3)
    w_z(4)
    w_core(5)
    w_core(6)
    q_f(7)
    for i in range(8):
        q_f_wait(i)
    w_z_wait(4)
    w_core(7)
    own_q.wait()
    own_w.wait()
    for i in range(8):
        zz = (z + OFFS[i]) % NZ
        arrived(ws_ref.at[zz, 1 - c], v_s.at[i], v_r.at[i])
        for j in range(4):
            arrived(qs_ref.at[1 - c, (y + j) % NY, zz], c_s.at[8 * j + i], c_r.at[8 * j + i])
    last = pltpu.make_async_copy(qs_ref.at[:, :, :, rows - 1], last_ref, own_sem.at[0])
    last.start()
    for d in sends:
        d.wait_send()
    last.wait()


def gather(q, wt):
    dma = pltpu.SemaphoreType.DMA
    anyspec = pl.BlockSpec(memory_space=pl.ANY)
    return pl.pallas_call(
        gather_kernel,
        out_shape=(
            pltpu.VMEM((NC, NY, NZ) + q.shape, q.dtype),
            pltpu.VMEM((NZ, NC) + wt.shape, wt.dtype),
            pltpu.VMEM((NC, NY, NZ) + q.shape[1:], q.dtype),
        ),
        in_specs=[anyspec] * 2,
        out_specs=(anyspec,) * 3,
        scratch_shapes=[dma((n,)) for n in (2, 8, 8, 16, 16, 16, 16, 32, 32, 8, 8, 8, 8)],
        compiler_params=pltpu.CompilerParams(collective_id=0, has_side_effects=True, vmem_limit_bytes=2**20),
        name="gather",
    )(q, wt)


NEG = -1e30
CHUNK = 64
BATCH = 32
ROWS = 2048
GROUPS = 24


def with_ids(queries, span_ids):
    flat = span_ids.T
    picks, rows = flat.shape
    tile = jnp.concatenate([flat // 32, flat % 32, jnp.zeros((picks, 128 - 2 * rows), jnp.int32)], axis=1)
    return jnp.concatenate([queries, tile.astype(queries.dtype)[None]], axis=0)


def list_requests(last_ref, slot_ref, first_ref, second_ref, lists_ref, counts_ref):
    spans = counts_ref.shape[0]
    me = lax.axis_index("pool")
    slots = slot_ref[...]
    where_id = lax.broadcasted_iota(jnp.int32, slots.shape, 0) * 128 + lax.broadcasted_iota(jnp.int32, slots.shape, 1)
    names = []
    for s in range(spans):
        found = jnp.where(slots == me * spans + s, where_id, 0).astype(jnp.float32)
        found = jnp.sum(found, axis=0, keepdims=True)
        names.append(jnp.broadcast_to(jnp.sum(found, axis=1, keepdims=True), (16, 128)))
    lane = lax.broadcasted_iota(jnp.int32, (8, 128), 1)
    sub = lax.broadcasted_iota(jnp.int32, (8, 128), 0)
    none = 1000

    def block(b, _):
        t = last_ref[b].astype(jnp.float32)
        ids = t * 32.0 + pltpu.roll(t, 96, 1)
        named = jnp.zeros((8, 128), jnp.float32)
        for s in range(spans):
            hit = jnp.where(ids == names[s], 1.0, 0.0)
            hit = jnp.max(hit, axis=0, keepdims=True)
            named = jnp.where(sub == s, jnp.broadcast_to(hit, (8, 128)), named)
        hit = (named > 0.0) & (lane < 32)
        low = jnp.min(jnp.where(hit, lane, none).astype(jnp.float32), axis=1, keepdims=True)
        high = jnp.max(jnp.where(hit, lane, -1).astype(jnp.float32), axis=1, keepdims=True)
        at = pl.ds(pl.multiple_of(b * 8, 8), 8)
        first_ref[at] = jnp.broadcast_to(low, (8, 128))
        second_ref[at] = jnp.broadcast_to(jnp.where(high > low, high, float(none)), (8, 128))
        return 0

    blocks = last_ref.shape[0]
    lax.fori_loop(0, blocks, block, 0, unroll=4)
    b = lax.broadcasted_iota(jnp.int32, (blocks, 128), 0)
    k = lax.broadcasted_iota(jnp.int32, (blocks, 128), 1).astype(jnp.float32)
    z, y, c = b % NZ, b // NZ % NY, b // (NZ * NY)
    early = c * 512 + (z * NY + y) * HR
    late = ROWS // 2 + c * 512 + (y * NZ + z) * HR - HR
    below = jnp.where(lax.broadcasted_iota(jnp.int32, (blocks, blocks), 0) > lax.broadcasted_iota(jnp.int32, (blocks, blocks), 1), 1.0, 0.0).astype(jnp.bfloat16)
    for s in range(spans):
        count = jnp.zeros((1, 128), jnp.float32)
        listing = jnp.zeros((1, 128), jnp.int32)
        for ref in (first_ref, second_ref):
            row = ref[pl.ds(s, blocks, stride=8), :]
            used = row < 32.0
            one = jnp.where(used, 1.0, 0.0)
            rank = jnp.dot(below, one.astype(jnp.bfloat16), preferred_element_type=jnp.float32) + count
            r = row.astype(jnp.int32)
            place = jnp.where(r < HR, early, late) + r + 4096 * (b * 33 + r)
            listing += jnp.sum(jnp.where(used & (rank == k), place, 0), axis=0, keepdims=True)
            count += jnp.sum(one, axis=0, keepdims=True)
        lists_ref[spans:spans + 8, :] = jnp.full((8, 128), ROWS, jnp.int32)
        lists_ref[s:s + 1, :] = jnp.where(lane[0:1].astype(jnp.float32) < count, listing, ROWS)
        counts_ref[s:s + 1, :] = count.astype(jnp.int32)


def attend_kernel(last_ref, slot_ref, q_ref, k_hbm, v_hbm, d_ref, st_ref, first_ref, second_ref, lists_ref, counts_ref, list_ref, count_ref, lsem, kbuf, vbuf, l0, l1, p0, p1, e0, e1, ksem, vsem):
    spans = kbuf.shape[0]
    for s in range(spans):
        for hbm, buf, sem in ((k_hbm, kbuf, ksem), (v_hbm, vbuf, vsem)):
            d = pltpu.make_async_copy(hbm.at[s], buf.at[s], sem.at[s])
            d.start()

    list_requests(last_ref, slot_ref, first_ref, second_ref, lists_ref, counts_ref)
    moves = [pltpu.make_async_copy(lists_ref, list_ref, lsem.at[0]), pltpu.make_async_copy(counts_ref, count_ref, lsem.at[1])]
    for d in moves:
        d.start()

    def clear(i, _):
        d_ref[pl.ds(i * 8, 8)] = jnp.zeros((8, 16, 128), jnp.bfloat16)
        return 0

    lax.fori_loop(0, ROWS // 8 + 1, clear, 0)
    st_ref[...] = jnp.full(st_ref.shape, NEG, jnp.float32)
    for d in moves:
        d.wait()
    scale2 = math.log2(math.e) / math.sqrt(HD)
    lane = lax.broadcasted_iota(jnp.int32, (16, 128), 1)

    def compute(s, base, slot):
        for i in range(0, CHUNK, 2):
            a = q_ref[list_ref[s, base + i] >> 12].astype(jnp.float32)
            b = q_ref[list_ref[s, base + i + 1] >> 12].astype(jnp.float32)
            l0[pl.ds(i * 8, 16)] = jnp.concatenate([a[0:8], b[0:8]], axis=0).astype(jnp.bfloat16)
            l1[pl.ds(i * 8, 16)] = jnp.concatenate([a[8:16], b[8:16]], axis=0).astype(jnp.bfloat16)
        scores = []
        for kv, l in enumerate((l0, l1)):
            keys = kbuf[s, :, kv * HD:(kv + 1) * HD]
            scores.append(lax.dot_general(l[...], keys, (((1,), (1,)), ((), ())), preferred_element_type=jnp.float32) * scale2)
        for kv, (p, e) in enumerate(((p0, e0), (p1, e1))):
            sc = scores[kv]
            vals = vbuf[s, :, kv * HD:(kv + 1) * HD]
            m = jnp.max(sc, axis=1, keepdims=True)
            ex = jnp.exp2(sc - m)
            tot = jnp.sum(ex, axis=1, keepdims=True)
            pv = jnp.dot(ex.astype(jnp.bfloat16), vals, preferred_element_type=jnp.float32)
            p[slot] = pv * (1.0 / tot)
            e[slot] = jnp.broadcast_to(m + jnp.log2(tot), e.shape[1:])

    def fold(s, base, slot):
        for first in range(0, CHUNK, BATCH):
            done = []
            for i in range(first, first + BATCH):
                place = list_ref[s, base + i] & 4095
                early = place < ROWS // 2
                g = jnp.where(early, place >> 6, 8 + (place >> 7))
                at = place & jnp.where(early, 63, 127)
                here = lane == at
                new = jnp.concatenate([p0[slot, pl.ds(i * 8, 8)], p1[slot, pl.ds(i * 8, 8)]], axis=0)
                le = jnp.concatenate([e0[slot, pl.ds(i * 8, 8)], e1[slot, pl.ds(i * 8, 8)]], axis=0)
                old = d_ref[place].astype(jnp.float32)
                ol = jnp.max(jnp.where(here, st_ref[g], -3e38), axis=1, keepdims=True)
                ex = jnp.exp2(-jnp.abs(le - ol))
                both = 1.0 + ex
                w = jnp.where(le > ol, 1.0, ex) / both
                done.append((place, g, here, old + w * (new - old), jnp.maximum(le, ol) + jnp.log2(both)))
            for place, g, here, tile, le in done:
                d_ref[place] = tile.astype(jnp.bfloat16)
            for place, g, here, tile, le in done:
                st_ref[g] = jnp.where(here, le, st_ref[g])

    total = jnp.int32(0)
    for s in range(spans):
        total += jnp.maximum((count_ref[s, 0] + CHUNK - 1) // CHUNK, 1)

    def step(t, carry):
        s, base, s_before, base_before = carry

        @pl.when(base == 0)
        def _():
            pltpu.make_async_copy(k_hbm.at[s], kbuf.at[s], ksem.at[s]).wait()
            pltpu.make_async_copy(v_hbm.at[s], vbuf.at[s], vsem.at[s]).wait()

        slot = t % 2
        compute(s, base, slot)
        fold(s_before, base_before, 1 - slot)
        more = base + CHUNK < count_ref[s, 0]
        return jnp.where(more, s, s + 1), jnp.where(more, base + CHUNK, 0), s, base

    zero = jnp.int32(0)
    _, _, s, base = lax.fori_loop(0, total, step, (zero, zero, jnp.int32(spans), zero))
    fold(s, base, (total - 1) % 2)


def attend(last, span_slot, qs, span_keys, span_values):
    anyspec = pl.BlockSpec(memory_space=pl.ANY)
    vmem = pl.BlockSpec(memory_space=pltpu.VMEM)
    rows = CHUNK * 8
    spans = span_keys.shape[0]
    blocks = NC * NY * NZ
    return pl.pallas_call(
        attend_kernel,
        out_shape=(pltpu.VMEM((ROWS + 8, 16, HD), jnp.bfloat16), pltpu.VMEM((GROUPS + 1, 16, 128), jnp.float32)),
        in_specs=[vmem, vmem, vmem, anyspec, anyspec],
        out_specs=(vmem, vmem),
        scratch_shapes=[pltpu.VMEM((blocks * 8, 128), jnp.float32)] * 2
        + [pltpu.VMEM((spans + 8, 128), jnp.int32), pltpu.VMEM((spans, 128), jnp.int32)]
        + [pltpu.SMEM((spans + 8, 128), jnp.int32), pltpu.SMEM((spans, 128), jnp.int32)]
        + [pltpu.SemaphoreType.DMA((2,))]
        + [pltpu.VMEM(span_keys.shape, jnp.bfloat16)] * 2
        + [pltpu.VMEM((rows, HD), jnp.bfloat16)] * 2
        + [pltpu.VMEM((2, rows, HD), jnp.float32)] * 4
        + [pltpu.SemaphoreType.DMA((spans,))] * 2,
        compiler_params=pltpu.CompilerParams(vmem_limit_bytes=24 * 2**20),
        name="attend",
    )(
        last.reshape(blocks, 16, 128),
        span_slot.reshape(-1, 128),
        pltpu.with_memory_space_constraint(qs.reshape(-1, 16, HD), pltpu.VMEM),
        pltpu.with_memory_space_constraint(span_keys, pltpu.HBM),
        pltpu.with_memory_space_constraint(span_values, pltpu.HBM),
    )


def merge_kernel(d_ref, st_ref, w_ref, out_ref,
                 ma, mb, ra, rb, sa, sb, rsa, rsb,
                 ua, da, usa, dsa, ub, db, usb, dsb, ya, ysa, uz, dz, usz, dsz,
                 fa, near, terms, xin, tsum, fin,
                 n_s, n_r, t_s, t_r, g_s, g_r,
                 own_sem, sib_s, sib_r, ua_s, ua_r, da_s, da_r, usa_s, usa_r, dsa_s, dsa_r,
                 ub_s, ub_r, db_s, db_r, usb_s, usb_r, dsb_s, dsb_r,
                 ya_s, ya_r, ysa_s, ysa_r, uz_s, uz_r, dz_s, dz_r, usz_s, usz_r, dsz_s, dsz_r):
    y, z, c = coords()
    zup, zdn = pid(y, z + 1, c), pid(y, z + NZ - 1, c)
    yup, ydn = pid(y + 1, z, c), pid(y + NY - 1, z, c)
    sib = pid(y, z, 1 - c)
    lane = lax.broadcasted_iota(jnp.int32, (16, 128), 1)

    x = lax.axis_index("head")

    def d_a(core, w):
        return d_ref.at[pl.ds(core * 512 + w * (NY * HR), NY * HR)]

    def d_b(core, w):
        return d_ref.at[pl.ds(ROWS // 2 + core * 512 + w * (NZ * HR), NZ * HR)]

    loads = [
        pltpu.make_async_copy(st_ref.at[pl.ds(c * NZ, NZ)], sa, own_sem.at[0]),
        pltpu.make_async_copy(st_ref.at[pl.ds(2 * NZ + c * NY, NY)], sb, own_sem.at[1]),
    ]
    for d in loads:
        d.start()
    barrier = pltpu.get_barrier_semaphore()
    for peer in (pid(y + 1, z, c), pid(y + 2, z, c), pid(y + 3, z, c), zup, zdn, sib):
        pl.semaphore_signal(barrier, inc=1, device_id={"pool": peer, "head": x}, device_id_type=MESH)
    me = pid(y, z, c)
    for d in (1, 2, 3):
        pl.semaphore_signal(barrier, inc=1, device_id={"pool": me, "head": (x + d) % NX}, device_id_type=MESH)
    flip = {"pool": pid(x, z, c), "head": y}

    @pl.when(x != y)
    def _():
        pl.semaphore_signal(barrier, inc=1, device_id=flip, device_id_type=MESH)
        pl.semaphore_wait(barrier, 10)

    @pl.when(x == y)
    def _():
        pl.semaphore_wait(barrier, 9)

    sends = []

    def send(src, dst, ss, rs, to, head=x):
        d = pltpu.make_async_remote_copy(src_ref=src, dst_ref=dst, send_sem=ss, recv_sem=rs, device_id={"pool": to, "head": head}, device_id_type=MESH)
        d.start()
        sends.append(d)

    def arrived(dst, ss, rs):
        pltpu.make_async_remote_copy(src_ref=dst, dst_ref=dst, send_sem=ss, recv_sem=rs, device_id={"pool": sib}, device_id_type=MESH).wait_recv()

    def zz(d):
        return (z + d + NZ) % NZ

    def yy(d):
        return (y + d + NY) % NY

    a_order = [4, 3, -3, 2, -2, 1, -1, 0]
    b_order = [2, 1, -1, 0]
    send(st_ref.at[pl.ds((1 - c) * NZ, NZ)], rsa, sib_s.at[12], sib_r.at[12], sib)
    send(st_ref.at[pl.ds(2 * NZ + (1 - c) * NY, NY)], rsb, sib_s.at[13], sib_r.at[13], sib)

    def sib_a(i):
        w = zz(a_order[i])
        send(d_a(1 - c, w), ra.at[w], sib_s.at[i], sib_r.at[i], sib)

    def sib_b(i):
        w = yy(b_order[i])
        send(d_b(1 - c, w), rb.at[w], sib_s.at[8 + i], sib_r.at[8 + i], sib)

    sib_a(0)
    sib_b(0)
    sib_a(1)
    sib_a(2)
    sib_b(1)
    sib_b(2)
    sib_a(3)
    sib_a(4)
    sib_a(5)
    sib_a(6)
    sib_b(3)
    sib_a(7)

    def blend(dst, src, wt, rows=HR, start=0, base=None):
        base = dst if base is None else base
        for i in range(start, start + rows):
            w = jnp.broadcast_to(wt[:, i:i + 1], (16, 128))
            a = base[i].astype(jnp.float32)
            b = src[i].astype(jnp.float32)
            dst[i] = (a + w * (b - a)).astype(jnp.bfloat16)

    def join(own, other):
        top = jnp.maximum(own, other)
        low = jnp.minimum(own, other)
        new = top + jnp.log2(1.0 + jnp.exp2(low - top))
        return new, jnp.exp2(other - new)

    def turned(wt, by):
        return pltpu.roll(wt, (128 - by) % 128, 1)

    for d in loads:
        d.wait()
    arrived(rsa, sib_s.at[12], sib_r.at[12])
    arrived(rsb, sib_s.at[13], sib_r.at[13])

    def core_a(i):
        w = zz(a_order[i])
        arrived(ra.at[w], sib_s.at[i], sib_r.at[i])
        new, wt = join(sa[w], rsa[w])
        sa[w] = new

        def cell(j, wt):
            part = pl.ds(j * HR, HR)
            blend(ma.at[w, j], ra.at[w, part], wt, base=d_a(c, w).at[part])
            return pltpu.roll(wt, 128 - HR, 1)

        lax.fori_loop(0, NY, cell, wt)

    def core_b(i):
        w = yy(b_order[i])
        arrived(rb.at[w], sib_s.at[8 + i], sib_r.at[8 + i])
        new, wt = join(sb[w], rsb[w])
        sb[w] = new

        def cell(j, wt):
            part = pl.ds(j * HR, HR)
            blend(mb.at[w, j], rb.at[w, part], wt, base=d_b(c, w).at[part])
            return pltpu.roll(wt, 128 - HR, 1)

        lax.fori_loop(0, NZ, cell, wt)

    a_up, a_dn = (2, 3, 0, 1), (0, 1, 2, 3)
    a_wt = {}

    def a_first():
        w = zz(4)
        for i in (0, 1):
            send(ma.at[w, i], ua.at[0, i], ua_s.at[i], ua_r.at[i], zup)
            send(ma.at[w, 2 + i], da.at[0, 2 + i], da_s.at[2 + i], da_r.at[2 + i], zdn)
        st = sa[w]
        usa[4] = jnp.where(lane < 2 * HR, st, NEG)
        dsa[4] = jnp.where(lane < 2 * HR, NEG, st)
        send(usa.at[4], usa.at[0], usa_s.at[0], usa_r.at[0], zup)
        send(dsa.at[4], dsa.at[0], dsa_s.at[0], dsa_r.at[0], zdn)

    def a_stat(k):
        wu, wd = zz(4 - k), zz(k - 4)
        arrived(usa.at[k - 1], usa_s.at[k - 1], usa_r.at[k - 1])
        own = sa[wu]
        newu, wtu = join(own, usa[k - 1])
        sa[wu] = newu
        if k < 4:
            send(sa.at[wu], usa.at[k], usa_s.at[k], usa_r.at[k], zup)
        arrived(dsa.at[k - 1], dsa_s.at[k - 1], dsa_r.at[k - 1])
        newd, wtd = join(sa[wd], dsa[k - 1])
        sa[wd] = newd
        if k < 4:
            send(sa.at[wd], dsa.at[k], dsa_s.at[k], dsa_r.at[k], zdn)
        if k == 4:
            early, wtd1 = join(own, dsa[k - 1])
            _, wtu2 = join(early, usa[k - 1])
            wtu = jnp.where(lane < 2 * HR, wtu2, wtu)
            wtd = jnp.where(lane < 2 * HR, wtd1, wtd)
        a_wt[k] = (wtu, wtd)

    def a_cell(k, i):
        wu, wd = zz(4 - k), zz(k - 4)
        for j, w, buf, ss, rs, to, t, has in (
            (a_up[i], wu, ua, ua_s, ua_r, zup, 0, k > 1 or a_up[i] < 2),
            (a_dn[i], wd, da, da_s, da_r, zdn, 1, k > 1 or a_dn[i] >= 2),
        ):
            n = 4 * (k - 1) + j
            if has:
                arrived(buf.at[k - 1, j], ss.at[n], rs.at[n])
                blend(ma.at[w, j], buf.at[k - 1, j], turned(a_wt[k][t], HR * j))
            if k < 4:
                send(ma.at[w, j], buf.at[k, j], ss.at[n + 4], rs.at[n + 4], to)

    b_up, b_dn = (4, 5, 6, 7, 0, 1, 2, 3), (0, 1, 2, 3, 4, 5, 6, 7)
    b_wt = {}

    def b_first():
        w = yy(2)
        for j in range(4):
            send(mb.at[w, j], ub.at[0, j], ub_s.at[j], ub_r.at[j], yup)
            send(mb.at[w, 4 + j], db.at[0, 4 + j], db_s.at[4 + j], db_r.at[4 + j], ydn)
        st = sb[w]
        usb[2] = jnp.where(lane < 4 * HR, st, NEG)
        dsb[2] = jnp.where(lane < 4 * HR, NEG, st)
        send(usb.at[2], usb.at[0], usb_s.at[0], usb_r.at[0], yup)
        send(dsb.at[2], dsb.at[0], dsb_s.at[0], dsb_r.at[0], ydn)

    def b_stat(k):
        wu, wd = yy(2 - k), yy(k - 2)
        arrived(usb.at[k - 1], usb_s.at[k - 1], usb_r.at[k - 1])
        own = sb[wu]
        newu, wtu = join(own, usb[k - 1])
        sb[wu] = newu
        if k < 2:
            send(sb.at[wu], usb.at[k], usb_s.at[k], usb_r.at[k], yup)
        arrived(dsb.at[k - 1], dsb_s.at[k - 1], dsb_r.at[k - 1])
        newd, wtd = join(sb[wd], dsb[k - 1])
        sb[wd] = newd
        if k < 2:
            send(sb.at[wd], dsb.at[k], dsb_s.at[k], dsb_r.at[k], ydn)
        if k == 2:
            early, wtd1 = join(own, dsb[k - 1])
            _, wtu2 = join(early, usb[k - 1])
            wtu = jnp.where(lane < 4 * HR, wtu2, wtu)
            wtd = jnp.where(lane < 4 * HR, wtd1, wtd)
        b_wt[k] = (wtu, wtd)

    def b_cell(k, i):
        wu, wd = yy(2 - k), yy(k - 2)
        for j, w, buf, ss, rs, to, t, has in (
            (b_up[i], wu, ub, ub_s, ub_r, yup, 0, k > 1 or b_up[i] < 4),
            (b_dn[i], wd, db, db_s, db_r, ydn, 1, k > 1 or b_dn[i] >= 4),
        ):
            n = 8 * (k - 1) + j
            if has:
                arrived(buf.at[k - 1, j], ss.at[n], rs.at[n])
                blend(mb.at[w, j], buf.at[k - 1, j], turned(b_wt[k][t], HR * j))
            if k < 2:
                send(mb.at[w, j], buf.at[k, j], ss.at[n + 8], rs.at[n + 8], to)

    def a_y():
        for d in (1, 2, 3):
            w = yy(d)
            send(sa.at[z], ysa.at[d - 1], ysa_s.at[d - 1], ysa_r.at[d - 1], pid(y + d, z, c))
            send(ma.at[z, w], ya.at[d - 1], ya_s.at[d - 1], ya_r.at[d - 1], pid(y + d, z, c))

    def a_y_end():
        total = turned(sa[z], HR * y)
        for d in (1, 3, 2):
            arrived(ysa.at[d - 1], ysa_s.at[d - 1], ysa_r.at[d - 1])
            total, wt = join(total, turned(ysa[d - 1], HR * y))
            arrived(ya.at[d - 1], ya_s.at[d - 1], ya_r.at[d - 1])
            blend(ma.at[z, y], ya.at[d - 1], wt)

    def bz_first():
        w = zz(4)
        usz[4] = turned(sb[y], HR * w)
        send(usz.at[4], usz.at[0], usz_s.at[0], usz_r.at[0], zup)
        send(usz.at[4], dsz.at[0], dsz_s.at[0], dsz_r.at[0], zdn)
        lo, hi = pl.ds(0, HR // 2), pl.ds(HR // 2, HR // 2)
        send(mb.at[y, w, lo], uz.at[0, lo], uz_s.at[0], uz_r.at[0], zup)
        send(mb.at[y, w, hi], dz.at[0, hi], dz_s.at[0], dz_r.at[0], zdn)

    def bz_step(k):
        wu, wd = zz(4 - k), zz(k - 4)
        lo, hi = pl.ds(0, HR // 2), pl.ds(HR // 2, HR // 2)
        arrived(usz.at[k - 1], usz_s.at[k - 1], usz_r.at[k - 1])
        ru = usz[k - 1]
        if k == 1:
            ru = jnp.where(lane < HR // 2, ru, NEG)
        newu, wtu = join(turned(sb[y], HR * wu), ru)
        if k < 4:
            usz[4 + k] = newu
            send(usz.at[4 + k], usz.at[k], usz_s.at[k], usz_r.at[k], zup)
        arrived(dsz.at[k - 1], dsz_s.at[k - 1], dsz_r.at[k - 1])
        rd = dsz[k - 1]
        if k == 1:
            rd = jnp.where(lane < HR // 2, NEG, rd)
        own = turned(sb[y], HR * wd) if k < 4 else newu
        newd, wtd = join(own, rd)
        if k < 4:
            dsz[4 + k] = newd
            send(dsz.at[4 + k], dsz.at[k], dsz_s.at[k], dsz_r.at[k], zdn)
        if k == 1:
            arrived(uz.at[0, lo], uz_s.at[0], uz_r.at[0])
            blend(mb.at[y, wu], uz.at[0], wtu, HR // 2, 0)
        else:
            arrived(uz.at[k - 1], uz_s.at[k - 1], uz_r.at[k - 1])
            blend(mb.at[y, wu], uz.at[k - 1], wtu)
        if k < 4:
            send(mb.at[y, wu], uz.at[k], uz_s.at[k], uz_r.at[k], zup)
        if k == 1:
            arrived(dz.at[0, hi], dz_s.at[0], dz_r.at[0])
            blend(mb.at[y, wd], dz.at[0], wtd, HR // 2, HR // 2)
        else:
            arrived(dz.at[k - 1], dz_s.at[k - 1], dz_r.at[k - 1])
            blend(mb.at[y, wd], dz.at[k - 1], wtd)
        if k < 4:
            send(mb.at[y, wd], dz.at[k], dz_s.at[k], dz_r.at[k], zdn)

    def share(h, cell):
        fa[...] = cell[...].astype(jnp.float32).reshape(HR * 16, HD)
        for i in range(16):
            near[h, y, :, i * HD:(i + 1) * HD] = fa[pl.ds(i, HR, stride=16), :].astype(jnp.bfloat16)
        for d in (1, 2, 3):
            n = 3 * h + d - 1
            send(near.at[h, y], near.at[h, y], n_s.at[n], n_r.at[n], pid(y + d, z, c))

    def project(h):
        for d in (1, 3, 2):
            n = 3 * h + d - 1
            arrived(near.at[h, yy(-d)], n_s.at[n], n_r.at[n])
        rows = near[h].reshape(NY * HR, near.shape[-1])
        wide = w_ref.shape[0]
        for lo in range(0, wide, 256):
            t = lax.dot_general(rows, w_ref[lo:lo + 256, :], (((1,), (1,)), ((), ())), preferred_element_type=jnp.float32)
            terms[h, :, :, lo:lo + 256] = t.astype(jnp.bfloat16).reshape(NY, HR, 256)
        for d in (1, 2, 3):
            n = 3 * h + d - 1
            to = (x + d) % NX
            send(terms.at[h, to], xin.at[h, d - 1], t_s.at[n], t_r.at[n], me, to)

    def finish(h):
        total = terms[h, x].astype(jnp.float32)
        for d in (1, 3, 2):
            n = 3 * h + d - 1
            arrived(xin.at[h, d - 1], t_s.at[n], t_r.at[n])
            total += xin[h, d - 1].astype(jnp.float32)
        tsum[h] = total.astype(jnp.bfloat16)

        @pl.when(x != y)
        def _():
            pltpu.make_async_remote_copy(src_ref=tsum.at[h], dst_ref=fin.at[h], send_sem=g_s.at[h], recv_sem=g_r.at[h], device_id=flip, device_id_type=MESH).start()

    def land(h):
        @pl.when(x != y)
        def _():
            pltpu.make_async_remote_copy(src_ref=tsum.at[h], dst_ref=fin.at[h], send_sem=g_s.at[h], recv_sem=g_r.at[h], device_id=flip, device_id_type=MESH).wait()
            out_ref[pl.ds(h * HR, HR)] = fin[h]

        @pl.when(x == y)
        def _():
            out_ref[pl.ds(h * HR, HR)] = tsum[h]

    core_a(0)
    a_first()
    core_b(0)
    b_first()
    core_a(1)
    core_a(2)
    a_cell(1, 0)
    a_cell(1, 1)
    core_b(1)
    core_b(2)
    for i in range(4):
        b_cell(1, i)
    a_stat(1)
    a_cell(1, 2)
    a_cell(1, 3)
    core_a(3)
    core_a(4)
    b_stat(1)
    a_stat(2)
    for i in range(4):
        a_cell(2, i)
        b_cell(1, 4 + i)
    core_a(5)
    core_a(6)
    a_stat(3)
    core_b(3)
    b_stat(2)
    for i in range(4):
        a_cell(3, i)
        b_cell(2, i)
    core_a(7)
    a_stat(4)
    for i in range(4):
        b_cell(2, 4 + i)
        if i == 3:
            bz_first()
        a_cell(4, i)
    bz_step(1)
    a_y()
    bz_step(2)
    a_y_end()
    share(0, ma.at[z, y])
    bz_step(3)
    bz_step(4)
    share(1, mb.at[y, z])
    project(0)
    project(1)
    finish(0)
    finish(1)
    land(0)
    land(1)
    for d in sends:
        d.wait_send()


def merge(d, st, weight):
    dma = pltpu.SemaphoreType.DMA
    bf, f32 = jnp.bfloat16, jnp.float32

    def v(*shape, dtype=bf):
        return pltpu.VMEM(shape + (16, 128), dtype)

    anyspec = pl.BlockSpec(memory_space=pl.ANY)
    vmem = pl.BlockSpec(memory_space=pltpu.VMEM)
    sems = [6, 6, 6, 6, 2, 2]
    sems += [2, 14, 14, 16, 16, 16, 16, 4, 4, 4, 4, 16, 16, 16, 16, 2, 2, 2, 2, 3, 3, 3, 3, 4, 4, 4, 4, 4, 4, 4, 4]
    wide, deep = weight.shape
    return pl.pallas_call(
        merge_kernel,
        out_shape=jax.ShapeDtypeStruct((2 * HR, wide), bf),
        in_specs=[vmem, vmem, vmem],
        out_specs=vmem,
        scratch_shapes=[
            v(NZ, NY, HR), v(NY, NZ, HR), v(NZ, NY * HR), v(NY, NZ * HR),
            v(NZ, dtype=f32), v(NY, dtype=f32), v(NZ, dtype=f32), v(NY, dtype=f32),
            v(4, NY, HR), v(4, NY, HR), v(5, dtype=f32), v(5, dtype=f32),
            v(2, NZ, HR), v(2, NZ, HR), v(3, dtype=f32), v(3, dtype=f32),
            v(3, HR), v(3, dtype=f32),
            v(4, HR), v(4, HR), v(8, dtype=f32), v(8, dtype=f32),
            pltpu.VMEM((HR * 16, HD), f32),
            pltpu.VMEM((2, NY, HR, deep), bf),
            pltpu.VMEM((2, NY, HR, wide), bf),
            pltpu.VMEM((2, 3, HR, wide), bf),
            pltpu.VMEM((2, HR, wide), bf),
            pltpu.VMEM((2, HR, wide), bf),
        ] + [dma((n,)) for n in sems],
        compiler_params=pltpu.CompilerParams(collective_id=1, has_side_effects=True, vmem_limit_bytes=20 * 2**20),
        name="merge",
    )(d, st, pltpu.with_memory_space_constraint(weight, pltpu.VMEM))


def body(queries, span_keys, span_values, span_ids, span_slot, out_weight):
    rows, width = queries.shape
    qs, ws, last = gather(with_ids(queries.reshape(rows, width // HD, HD), span_ids), out_weight.T)
    d, st = attend(last, span_slot, qs, span_keys, span_values)
    return merge(d, st, ws.reshape(-1, width))


def solution(mesh):
    in_specs = (
        P("pool", "head"),
        P("pool", None, "head"),
        P("pool", None, "head"),
        P("pool", None),
        P(),
        P("head", "pool"),
    )
    return jax.shard_map(body, mesh=mesh, in_specs=in_specs, out_specs=P("pool", "head"), check_vma=False)
```

```python
import functools
import math

import jax
import jax.numpy as jnp
from jax import lax
from jax.experimental import pallas as pl
from jax.experimental.pallas import tpu as pltpu
from jax.sharding import PartitionSpec as P

NX, NY, NZ, NC = 4, 4, 8, 2
HR = 16
HD = 128
MESH = pl.DeviceIdType.MESH
OFFS = (0, NZ - 1, 1, NZ - 2, 2, NZ - 3, 3, 4)


def coords():
    p = lax.axis_index("pool")
    return p // (NZ * NC), (p // NC) % NZ, p % NC


def pid(y, z, c):
    return ((y % NY) * NZ + z % NZ) * NC + c


def gather_kernel(q_ref, w_ref, qs_ref, ws_ref, last_ref, own_sem, z_s, z_r, y_s, y_r, f_s, f_r, c_s, c_r, w_s, w_r, v_s, v_r):
    y, z, c = coords()
    zup, zdn = pid(y, z + 1, c), pid(y, z + NZ - 1, c)
    yu, yd = (y + 1) % NY, (y + NY - 1) % NY
    yup, ydn = pid(yu, z, c), pid(yd, z, c)
    sib = pid(y, z, 1 - c)
    barrier = pltpu.get_barrier_semaphore()
    for peer in (zup, zdn, yup, ydn, sib):
        pl.semaphore_signal(barrier, inc=1, device_id={"pool": peer}, device_id_type=MESH)
    pl.semaphore_wait(barrier, 5)
    sends = []

    def send(src, dst, ss, rs, to):
        d = pltpu.make_async_remote_copy(src_ref=src, dst_ref=dst, send_sem=ss, recv_sem=rs, device_id={"pool": to}, device_id_type=MESH)
        d.start()
        sends.append(d)

    def arrived(dst, ss, rs):
        pltpu.make_async_remote_copy(src_ref=dst, dst_ref=dst, send_sem=ss, recv_sem=rs, device_id={"pool": sib}, device_id_type=MESH).wait_recv()

    rows, wide = q_ref.shape[0], w_ref.shape[0]
    own_q = pltpu.make_async_copy(q_ref, qs_ref.at[c, y, z], own_sem.at[0])
    own_w = pltpu.make_async_copy(w_ref, ws_ref.at[z, c], own_sem.at[1])
    own_q.start()
    own_w.start()
    lo, hi = pl.ds(0, rows // 2), pl.ds(rows // 2, rows - rows // 2)
    wcut = wide // 32 * 16
    wlo, whi = pl.ds(0, wcut), pl.ds(wcut, wide - wcut)

    def q_z(k):
        iu, idn = (z + NZ - (k - 1)) % NZ, (z + k - 1) % NZ
        up = q_ref if k == 1 else qs_ref.at[c, y, iu]
        dn = q_ref if k == 1 else qs_ref.at[c, y, idn]
        if k < 4:
            send(up, qs_ref.at[c, y, iu], z_s.at[2 * k - 2], z_r.at[2 * k - 2], zup)
            send(dn, qs_ref.at[c, y, idn], z_s.at[2 * k - 1], z_r.at[2 * k - 1], zdn)
        else:
            send(up.at[lo], qs_ref.at[c, y, iu, lo], z_s.at[6], z_r.at[6], zup)
            send(dn.at[hi], qs_ref.at[c, y, idn, hi], z_s.at[7], z_r.at[7], zdn)

    def q_z_wait(k):
        iu, idn = (z + NZ - k) % NZ, (z + k) % NZ
        if k < 4:
            arrived(qs_ref.at[c, y, iu], z_s.at[2 * k - 2], z_r.at[2 * k - 2])
            arrived(qs_ref.at[c, y, idn], z_s.at[2 * k - 1], z_r.at[2 * k - 1])
        else:
            arrived(qs_ref.at[c, y, iu, lo], z_s.at[6], z_r.at[6])
            arrived(qs_ref.at[c, y, idn, hi], z_s.at[7], z_r.at[7])

    def w_z(k):
        iu, idn = (z + NZ - (k - 1)) % NZ, (z + k - 1) % NZ
        up = w_ref if k == 1 else ws_ref.at[iu, c]
        dn = w_ref if k == 1 else ws_ref.at[idn, c]
        if k < 4:
            send(up, ws_ref.at[iu, c], w_s.at[2 * k - 2], w_r.at[2 * k - 2], zup)
            send(dn, ws_ref.at[idn, c], w_s.at[2 * k - 1], w_r.at[2 * k - 1], zdn)
        else:
            send(up.at[wlo], ws_ref.at[iu, c, wlo], w_s.at[6], w_r.at[6], zup)
            send(dn.at[whi], ws_ref.at[idn, c, whi], w_s.at[7], w_r.at[7], zdn)

    def w_z_wait(k):
        iu, idn = (z + NZ - k) % NZ, (z + k) % NZ
        if k < 4:
            arrived(ws_ref.at[iu, c], w_s.at[2 * k - 2], w_r.at[2 * k - 2])
            arrived(ws_ref.at[idn, c], w_s.at[2 * k - 1], w_r.at[2 * k - 1])
        else:
            arrived(ws_ref.at[iu, c, wlo], w_s.at[6], w_r.at[6])
            arrived(ws_ref.at[idn, c, whi], w_s.at[7], w_r.at[7])

    def w_core(i):
        zz = (z + OFFS[i]) % NZ
        src = w_ref if i == 0 else ws_ref.at[zz, c]
        send(src, ws_ref.at[zz, c], v_s.at[i], v_r.at[i], sib)

    def q_core(j, i):
        yy, zz = (y + j) % NY, (z + OFFS[i]) % NZ
        src = q_ref if i == 0 and j == 0 else qs_ref.at[c, yy, zz]
        send(src, qs_ref.at[c, yy, zz], c_s.at[8 * j + i], c_r.at[8 * j + i], sib)

    def q_y(i):
        zz = (z + OFFS[i]) % NZ
        src = q_ref if i == 0 else qs_ref.at[c, y, zz]
        send(src, qs_ref.at[c, y, zz], y_s.at[2 * i], y_r.at[2 * i], yup)
        send(src, qs_ref.at[c, y, zz], y_s.at[2 * i + 1], y_r.at[2 * i + 1], ydn)
        q_core(0, i)

    def q_f(i):
        zz = (z + OFFS[i]) % NZ
        arrived(qs_ref.at[c, yd, zz], y_s.at[2 * i], y_r.at[2 * i])
        send(qs_ref.at[c, yd, zz, lo], qs_ref.at[c, yd, zz, lo], f_s.at[2 * i], f_r.at[2 * i], yup)
        arrived(qs_ref.at[c, yu, zz], y_s.at[2 * i + 1], y_r.at[2 * i + 1])
        send(qs_ref.at[c, yu, zz, hi], qs_ref.at[c, yu, zz, hi], f_s.at[2 * i + 1], f_r.at[2 * i + 1], ydn)
        q_core(1, i)
        q_core(3, i)

    def q_f_wait(i):
        zz, yo = (z + OFFS[i]) % NZ, (y + 2) % NY
        arrived(qs_ref.at[c, yo, zz, lo], f_s.at[2 * i], f_r.at[2 * i])
        arrived(qs_ref.at[c, yo, zz, hi], f_s.at[2 * i + 1], f_r.at[2 * i + 1])
        q_core(2, i)

    q_z(1)
    q_y(0)
    w_z(1)
    w_core(0)
    q_z_wait(1)
    q_z(2)
    q_y(1)
    q_y(2)
    q_f(0)
    q_z_wait(2)
    q_z(3)
    q_y(3)
    q_y(4)
    q_f(1)
    q_f(2)
    q_z_wait(3)
    q_z(4)
    q_y(5)
    q_y(6)
    w_z_wait(1)
    w_z(2)
    w_core(1)
    w_core(2)
    q_z_wait(4)
    q_y(7)
    q_f(3)
    q_f(4)
    w_z_wait(2)
    w_z(3)
    w_core(3)
    w_core(4)
    q_f(5)
    q_f(6)
    w_z_wait(3)
    w_z(4)
    w_core(5)
    w_core(6)
    q_f(7)
    for i in range(8):
        q_f_wait(i)
    w_z_wait(4)
    w_core(7)
    own_q.wait()
    own_w.wait()
    for i in range(8):
        zz = (z + OFFS[i]) % NZ
        arrived(ws_ref.at[zz, 1 - c], v_s.at[i], v_r.at[i])
        for j in range(4):
            arrived(qs_ref.at[1 - c, (y + j) % NY, zz], c_s.at[8 * j + i], c_r.at[8 * j + i])
    last = pltpu.make_async_copy(qs_ref.at[:, :, :, rows - 1], last_ref, own_sem.at[0])
    last.start()
    for d in sends:
        d.wait_send()
    last.wait()


def gather(q, wt):
    dma = pltpu.SemaphoreType.DMA
    anyspec = pl.BlockSpec(memory_space=pl.ANY)
    return pl.pallas_call(
        gather_kernel,
        out_shape=(
            pltpu.VMEM((NC, NY, NZ) + q.shape, q.dtype),
            pltpu.VMEM((NZ, NC) + wt.shape, wt.dtype),
            pltpu.VMEM((NC, NY, NZ) + q.shape[1:], q.dtype),
        ),
        in_specs=[anyspec] * 2,
        out_specs=(anyspec,) * 3,
        scratch_shapes=[dma((n,)) for n in (2, 8, 8, 16, 16, 16, 16, 32, 32, 8, 8, 8, 8)],
        compiler_params=pltpu.CompilerParams(collective_id=0, has_side_effects=True, vmem_limit_bytes=2**20),
        name="gather",
    )(q, pltpu.with_memory_space_constraint(wt, pltpu.HBM))


NEG = -1e30
CHUNK = 64
BATCH = 32
ROWS = 2048
GROUPS = 24


def with_ids(queries, span_ids):
    flat = span_ids.T
    picks, rows = flat.shape
    tile = jnp.concatenate([flat // 32, flat % 32, jnp.zeros((picks, 128 - 2 * rows), jnp.int32)], axis=1)
    return jnp.concatenate([queries, tile.astype(queries.dtype)[None]], axis=0)


def list_requests(last_ref, slot_ref, first_ref, second_ref, lists_ref, counts_ref):
    spans = counts_ref.shape[0]
    me = lax.axis_index("pool")
    slots = slot_ref[...]
    where_id = lax.broadcasted_iota(jnp.int32, slots.shape, 0) * 128 + lax.broadcasted_iota(jnp.int32, slots.shape, 1)
    names = []
    for s in range(spans):
        found = jnp.where(slots == me * spans + s, where_id, 0).astype(jnp.float32)
        found = jnp.sum(found, axis=0, keepdims=True)
        names.append(jnp.broadcast_to(jnp.sum(found, axis=1, keepdims=True), (16, 128)))
    lane = lax.broadcasted_iota(jnp.int32, (8, 128), 1)
    sub = lax.broadcasted_iota(jnp.int32, (8, 128), 0)
    none = 1000

    def block(b, _):
        t = last_ref[b].astype(jnp.float32)
        ids = t * 32.0 + pltpu.roll(t, 96, 1)
        named = jnp.zeros((8, 128), jnp.float32)
        for s in range(spans):
            hit = jnp.where(ids == names[s], 1.0, 0.0)
            hit = jnp.max(hit, axis=0, keepdims=True)
            named = jnp.where(sub == s, jnp.broadcast_to(hit, (8, 128)), named)
        hit = (named > 0.0) & (lane < 32)
        low = jnp.min(jnp.where(hit, lane, none).astype(jnp.float32), axis=1, keepdims=True)
        high = jnp.max(jnp.where(hit, lane, -1).astype(jnp.float32), axis=1, keepdims=True)
        at = pl.ds(pl.multiple_of(b * 8, 8), 8)
        first_ref[at] = jnp.broadcast_to(low, (8, 128))
        second_ref[at] = jnp.broadcast_to(jnp.where(high > low, high, float(none)), (8, 128))
        return 0

    blocks = last_ref.shape[0]
    lax.fori_loop(0, blocks, block, 0, unroll=4)
    b = lax.broadcasted_iota(jnp.int32, (blocks, 128), 0)
    k = lax.broadcasted_iota(jnp.int32, (blocks, 128), 1).astype(jnp.float32)
    z, y, c = b % NZ, b // NZ % NY, b // (NZ * NY)
    early = c * 512 + (z * NY + y) * HR
    late = ROWS // 2 + c * 512 + (y * NZ + z) * HR - HR
    below = jnp.where(lax.broadcasted_iota(jnp.int32, (blocks, blocks), 0) > lax.broadcasted_iota(jnp.int32, (blocks, blocks), 1), 1.0, 0.0).astype(jnp.bfloat16)
    for s in range(spans):
        count = jnp.zeros((1, 128), jnp.float32)
        listing = jnp.zeros((1, 128), jnp.int32)
        for ref in (first_ref, second_ref):
            row = ref[pl.ds(s, blocks, stride=8), :]
            used = row < 32.0
            one = jnp.where(used, 1.0, 0.0)
            rank = jnp.dot(below, one.astype(jnp.bfloat16), preferred_element_type=jnp.float32) + count
            r = row.astype(jnp.int32)
            place = jnp.where(r < HR, early, late) + r + 4096 * (b * 33 + r)
            listing += jnp.sum(jnp.where(used & (rank == k), place, 0), axis=0, keepdims=True)
            count += jnp.sum(one, axis=0, keepdims=True)
        lists_ref[spans:spans + 8, :] = jnp.full((8, 128), ROWS, jnp.int32)
        lists_ref[s:s + 1, :] = jnp.where(lane[0:1].astype(jnp.float32) < count, listing, ROWS)
        counts_ref[s:s + 1, :] = count.astype(jnp.int32)


def attend_kernel(last_ref, slot_ref, q_ref, k_hbm, v_hbm, d_ref, st_ref, first_ref, second_ref, lists_ref, counts_ref, list_ref, count_ref, lsem, kbuf, vbuf, l0, l1, p0, p1, e0, e1, ksem, vsem):
    spans = kbuf.shape[0]
    for s in range(spans):
        for hbm, buf, sem in ((k_hbm, kbuf, ksem), (v_hbm, vbuf, vsem)):
            d = pltpu.make_async_copy(hbm.at[s], buf.at[s], sem.at[s])
            d.start()

    list_requests(last_ref, slot_ref, first_ref, second_ref, lists_ref, counts_ref)
    moves = [pltpu.make_async_copy(lists_ref, list_ref, lsem.at[0]), pltpu.make_async_copy(counts_ref, count_ref, lsem.at[1])]
    for d in moves:
        d.start()

    def clear(i, _):
        d_ref[pl.ds(i * 8, 8)] = jnp.zeros((8, 16, 128), jnp.bfloat16)
        return 0

    lax.fori_loop(0, ROWS // 8 + 1, clear, 0)
    st_ref[...] = jnp.full(st_ref.shape, NEG, jnp.float32)
    for d in moves:
        d.wait()
    scale2 = math.log2(math.e) / math.sqrt(HD)
    lane = lax.broadcasted_iota(jnp.int32, (16, 128), 1)

    def compute(s, base, slot):
        for i in range(0, CHUNK, 2):
            a = q_ref[list_ref[s, base + i] >> 12].astype(jnp.float32)
            b = q_ref[list_ref[s, base + i + 1] >> 12].astype(jnp.float32)
            l0[pl.ds(i * 8, 16)] = jnp.concatenate([a[0:8], b[0:8]], axis=0).astype(jnp.bfloat16)
            l1[pl.ds(i * 8, 16)] = jnp.concatenate([a[8:16], b[8:16]], axis=0).astype(jnp.bfloat16)
        scores = []
        for kv, l in enumerate((l0, l1)):
            keys = kbuf[s, :, kv * HD:(kv + 1) * HD]
            scores.append(lax.dot_general(l[...], keys, (((1,), (1,)), ((), ())), preferred_element_type=jnp.float32) * scale2)
        for kv, (p, e) in enumerate(((p0, e0), (p1, e1))):
            sc = scores[kv]
            vals = vbuf[s, :, kv * HD:(kv + 1) * HD]
            m = jnp.max(sc, axis=1, keepdims=True)
            ex = jnp.exp2(sc - m)
            tot = jnp.sum(ex, axis=1, keepdims=True)
            pv = jnp.dot(ex.astype(jnp.bfloat16), vals, preferred_element_type=jnp.float32)
            p[slot] = pv * (1.0 / tot)
            e[slot] = jnp.broadcast_to(m + jnp.log2(tot), e.shape[1:])

    def fold(s, base, slot):
        for first in range(0, CHUNK, BATCH):
            done = []
            for i in range(first, first + BATCH):
                place = list_ref[s, base + i] & 4095
                early = place < ROWS // 2
                g = jnp.where(early, place >> 6, 8 + (place >> 7))
                at = place & jnp.where(early, 63, 127)
                here = lane == at
                new = jnp.concatenate([p0[slot, pl.ds(i * 8, 8)], p1[slot, pl.ds(i * 8, 8)]], axis=0)
                le = jnp.concatenate([e0[slot, pl.ds(i * 8, 8)], e1[slot, pl.ds(i * 8, 8)]], axis=0)
                old = d_ref[place].astype(jnp.float32)
                ol = jnp.max(jnp.where(here, st_ref[g], -3e38), axis=1, keepdims=True)
                ex = jnp.exp2(-jnp.abs(le - ol))
                both = 1.0 + ex
                w = jnp.where(le > ol, 1.0, ex) / both
                done.append((place, g, here, old + w * (new - old), jnp.maximum(le, ol) + jnp.log2(both)))
            for place, g, here, tile, le in done:
                d_ref[place] = tile.astype(jnp.bfloat16)
            for place, g, here, tile, le in done:
                st_ref[g] = jnp.where(here, le, st_ref[g])

    total = jnp.int32(0)
    for s in range(spans):
        total += jnp.maximum((count_ref[s, 0] + CHUNK - 1) // CHUNK, 1)

    def step(t, carry):
        s, base, s_before, base_before = carry

        @pl.when(base == 0)
        def _():
            pltpu.make_async_copy(k_hbm.at[s], kbuf.at[s], ksem.at[s]).wait()
            pltpu.make_async_copy(v_hbm.at[s], vbuf.at[s], vsem.at[s]).wait()

        slot = t % 2
        compute(s, base, slot)
        fold(s_before, base_before, 1 - slot)
        more = base + CHUNK < count_ref[s, 0]
        return jnp.where(more, s, s + 1), jnp.where(more, base + CHUNK, 0), s, base

    zero = jnp.int32(0)
    _, _, s, base = lax.fori_loop(0, total, step, (zero, zero, jnp.int32(spans), zero))
    fold(s, base, (total - 1) % 2)


def attend(last, span_slot, qs, span_keys, span_values):
    anyspec = pl.BlockSpec(memory_space=pl.ANY)
    vmem = pl.BlockSpec(memory_space=pltpu.VMEM)
    rows = CHUNK * 8
    spans = span_keys.shape[0]
    blocks = NC * NY * NZ
    return pl.pallas_call(
        attend_kernel,
        out_shape=(pltpu.VMEM((ROWS + 8, 16, HD), jnp.bfloat16), pltpu.VMEM((GROUPS + 1, 16, 128), jnp.float32)),
        in_specs=[vmem, vmem, vmem, anyspec, anyspec],
        out_specs=(vmem, vmem),
        scratch_shapes=[pltpu.VMEM((blocks * 8, 128), jnp.float32)] * 2
        + [pltpu.VMEM((spans + 8, 128), jnp.int32), pltpu.VMEM((spans, 128), jnp.int32)]
        + [pltpu.SMEM((spans + 8, 128), jnp.int32), pltpu.SMEM((spans, 128), jnp.int32)]
        + [pltpu.SemaphoreType.DMA((2,))]
        + [pltpu.VMEM(span_keys.shape, jnp.bfloat16)] * 2
        + [pltpu.VMEM((rows, HD), jnp.bfloat16)] * 2
        + [pltpu.VMEM((2, rows, HD), jnp.float32)] * 4
        + [pltpu.SemaphoreType.DMA((spans,))] * 2,
        compiler_params=pltpu.CompilerParams(vmem_limit_bytes=24 * 2**20),
        name="attend",
    )(
        last.reshape(blocks, 16, 128),
        span_slot.reshape(-1, 128),
        pltpu.with_memory_space_constraint(qs.reshape(-1, 16, HD), pltpu.VMEM),
        pltpu.with_memory_space_constraint(span_keys, pltpu.HBM),
        pltpu.with_memory_space_constraint(span_values, pltpu.HBM),
    )


def merge_kernel(d_ref, st_ref, w_ref, out_ref,
                 ma, mb, ra, rb, sa, sb, rsa, rsb,
                 ua, da, usa, dsa, ub, db, usb, dsb, ya, ysa, uz, dz, usz, dsz,
                 fa, near, terms, xin, tsum, fin,
                 n_s, n_r, t_s, t_r, g_s, g_r,
                 own_sem, sib_s, sib_r, ua_s, ua_r, da_s, da_r, usa_s, usa_r, dsa_s, dsa_r,
                 ub_s, ub_r, db_s, db_r, usb_s, usb_r, dsb_s, dsb_r,
                 ya_s, ya_r, ysa_s, ysa_r, uz_s, uz_r, dz_s, dz_r, usz_s, usz_r, dsz_s, dsz_r):
    y, z, c = coords()
    zup, zdn = pid(y, z + 1, c), pid(y, z + NZ - 1, c)
    yup, ydn = pid(y + 1, z, c), pid(y + NY - 1, z, c)
    sib = pid(y, z, 1 - c)
    lane = lax.broadcasted_iota(jnp.int32, (16, 128), 1)

    x = lax.axis_index("head")

    def d_a(core, w):
        return d_ref.at[pl.ds(core * 512 + w * (NY * HR), NY * HR)]

    def d_b(core, w):
        return d_ref.at[pl.ds(ROWS // 2 + core * 512 + w * (NZ * HR), NZ * HR)]

    loads = [
        pltpu.make_async_copy(st_ref.at[pl.ds(c * NZ, NZ)], sa, own_sem.at[0]),
        pltpu.make_async_copy(st_ref.at[pl.ds(2 * NZ + c * NY, NY)], sb, own_sem.at[1]),
    ]
    for d in loads:
        d.start()
    barrier = pltpu.get_barrier_semaphore()
    for peer in (pid(y + 1, z, c), pid(y + 2, z, c), pid(y + 3, z, c), zup, zdn, sib):
        pl.semaphore_signal(barrier, inc=1, device_id={"pool": peer, "head": x}, device_id_type=MESH)
    me = pid(y, z, c)
    for d in (1, 2, 3):
        pl.semaphore_signal(barrier, inc=1, device_id={"pool": me, "head": (x + d) % NX}, device_id_type=MESH)
    flip = {"pool": pid(x, z, c), "head": y}

    @pl.when(x != y)
    def _():
        pl.semaphore_signal(barrier, inc=1, device_id=flip, device_id_type=MESH)
        pl.semaphore_wait(barrier, 10)

    @pl.when(x == y)
    def _():
        pl.semaphore_wait(barrier, 9)

    sends = []

    def send(src, dst, ss, rs, to, head=x):
        d = pltpu.make_async_remote_copy(src_ref=src, dst_ref=dst, send_sem=ss, recv_sem=rs, device_id={"pool": to, "head": head}, device_id_type=MESH)
        d.start()
        sends.append(d)

    def arrived(dst, ss, rs):
        pltpu.make_async_remote_copy(src_ref=dst, dst_ref=dst, send_sem=ss, recv_sem=rs, device_id={"pool": sib}, device_id_type=MESH).wait_recv()

    def zz(d):
        return (z + d + NZ) % NZ

    def yy(d):
        return (y + d + NY) % NY

    a_order = [4, 3, -3, 2, -2, 1, -1, 0]
    b_order = [2, 1, -1, 0]
    send(st_ref.at[pl.ds((1 - c) * NZ, NZ)], rsa, sib_s.at[12], sib_r.at[12], sib)
    send(st_ref.at[pl.ds(2 * NZ + (1 - c) * NY, NY)], rsb, sib_s.at[13], sib_r.at[13], sib)

    def sib_a(i):
        w = zz(a_order[i])
        send(d_a(1 - c, w), ra.at[w], sib_s.at[i], sib_r.at[i], sib)

    def sib_b(i):
        w = yy(b_order[i])
        send(d_b(1 - c, w), rb.at[w], sib_s.at[8 + i], sib_r.at[8 + i], sib)

    sib_a(0)
    sib_b(0)
    sib_a(1)
    sib_a(2)
    sib_b(1)
    sib_b(2)
    sib_a(3)
    sib_a(4)
    sib_a(5)
    sib_a(6)
    sib_b(3)
    sib_a(7)

    def blend(dst, src, wt, rows=HR, start=0, base=None):
        base = dst if base is None else base
        for i in range(start, start + rows):
            w = jnp.broadcast_to(wt[:, i:i + 1], (16, 128))
            a = base[i].astype(jnp.float32)
            b = src[i].astype(jnp.float32)
            dst[i] = (a + w * (b - a)).astype(jnp.bfloat16)

    def join(own, other):
        top = jnp.maximum(own, other)
        low = jnp.minimum(own, other)
        new = top + jnp.log2(1.0 + jnp.exp2(low - top))
        return new, jnp.exp2(other - new)

    def turned(wt, by):
        return pltpu.roll(wt, (128 - by) % 128, 1)

    for d in loads:
        d.wait()
    arrived(rsa, sib_s.at[12], sib_r.at[12])
    arrived(rsb, sib_s.at[13], sib_r.at[13])

    def core_a(i):
        w = zz(a_order[i])
        arrived(ra.at[w], sib_s.at[i], sib_r.at[i])
        new, wt = join(sa[w], rsa[w])
        sa[w] = new

        def cell(j, wt):
            part = pl.ds(j * HR, HR)
            blend(ma.at[w, j], ra.at[w, part], wt, base=d_a(c, w).at[part])
            return pltpu.roll(wt, 128 - HR, 1)

        lax.fori_loop(0, NY, cell, wt)

    def core_b(i):
        w = yy(b_order[i])
        arrived(rb.at[w], sib_s.at[8 + i], sib_r.at[8 + i])
        new, wt = join(sb[w], rsb[w])
        sb[w] = new

        def cell(j, wt):
            part = pl.ds(j * HR, HR)
            blend(mb.at[w, j], rb.at[w, part], wt, base=d_b(c, w).at[part])
            return pltpu.roll(wt, 128 - HR, 1)

        lax.fori_loop(0, NZ, cell, wt)

    a_up, a_dn = (2, 3, 0, 1), (0, 1, 2, 3)
    a_wt = {}

    def a_first():
        w = zz(4)
        for i in (0, 1):
            send(ma.at[w, i], ua.at[0, i], ua_s.at[i], ua_r.at[i], zup)
            send(ma.at[w, 2 + i], da.at[0, 2 + i], da_s.at[2 + i], da_r.at[2 + i], zdn)
        st = sa[w]
        usa[4] = jnp.where(lane < 2 * HR, st, NEG)
        dsa[4] = jnp.where(lane < 2 * HR, NEG, st)
        send(usa.at[4], usa.at[0], usa_s.at[0], usa_r.at[0], zup)
        send(dsa.at[4], dsa.at[0], dsa_s.at[0], dsa_r.at[0], zdn)

    def a_stat(k):
        wu, wd = zz(4 - k), zz(k - 4)
        arrived(usa.at[k - 1], usa_s.at[k - 1], usa_r.at[k - 1])
        own = sa[wu]
        newu, wtu = join(own, usa[k - 1])
        sa[wu] = newu
        if k < 4:
            send(sa.at[wu], usa.at[k], usa_s.at[k], usa_r.at[k], zup)
        arrived(dsa.at[k - 1], dsa_s.at[k - 1], dsa_r.at[k - 1])
        newd, wtd = join(sa[wd], dsa[k - 1])
        sa[wd] = newd
        if k < 4:
            send(sa.at[wd], dsa.at[k], dsa_s.at[k], dsa_r.at[k], zdn)
        if k == 4:
            early, wtd1 = join(own, dsa[k - 1])
            _, wtu2 = join(early, usa[k - 1])
            wtu = jnp.where(lane < 2 * HR, wtu2, wtu)
            wtd = jnp.where(lane < 2 * HR, wtd1, wtd)
        a_wt[k] = (wtu, wtd)

    def a_cell(k, i):
        wu, wd = zz(4 - k), zz(k - 4)
        for j, w, buf, ss, rs, to, t, has in (
            (a_up[i], wu, ua, ua_s, ua_r, zup, 0, k > 1 or a_up[i] < 2),
            (a_dn[i], wd, da, da_s, da_r, zdn, 1, k > 1 or a_dn[i] >= 2),
        ):
            n = 4 * (k - 1) + j
            if has:
                arrived(buf.at[k - 1, j], ss.at[n], rs.at[n])
                blend(ma.at[w, j], buf.at[k - 1, j], turned(a_wt[k][t], HR * j))
            if k < 4:
                send(ma.at[w, j], buf.at[k, j], ss.at[n + 4], rs.at[n + 4], to)

    b_up, b_dn = (4, 5, 6, 7, 0, 1, 2, 3), (0, 1, 2, 3, 4, 5, 6, 7)
    b_wt = {}

    def b_first():
        w = yy(2)
        for j in range(4):
            send(mb.at[w, j], ub.at[0, j], ub_s.at[j], ub_r.at[j], yup)
            send(mb.at[w, 4 + j], db.at[0, 4 + j], db_s.at[4 + j], db_r.at[4 + j], ydn)
        st = sb[w]
        usb[2] = jnp.where(lane < 4 * HR, st, NEG)
        dsb[2] = jnp.where(lane < 4 * HR, NEG, st)
        send(usb.at[2], usb.at[0], usb_s.at[0], usb_r.at[0], yup)
        send(dsb.at[2], dsb.at[0], dsb_s.at[0], dsb_r.at[0], ydn)

    def b_stat(k):
        wu, wd = yy(2 - k), yy(k - 2)
        arrived(usb.at[k - 1], usb_s.at[k - 1], usb_r.at[k - 1])
        own = sb[wu]
        newu, wtu = join(own, usb[k - 1])
        sb[wu] = newu
        if k < 2:
            send(sb.at[wu], usb.at[k], usb_s.at[k], usb_r.at[k], yup)
        arrived(dsb.at[k - 1], dsb_s.at[k - 1], dsb_r.at[k - 1])
        newd, wtd = join(sb[wd], dsb[k - 1])
        sb[wd] = newd
        if k < 2:
            send(sb.at[wd], dsb.at[k], dsb_s.at[k], dsb_r.at[k], ydn)
        if k == 2:
            early, wtd1 = join(own, dsb[k - 1])
            _, wtu2 = join(early, usb[k - 1])
            wtu = jnp.where(lane < 4 * HR, wtu2, wtu)
            wtd = jnp.where(lane < 4 * HR, wtd1, wtd)
        b_wt[k] = (wtu, wtd)

    def b_cell(k, i):
        wu, wd = yy(2 - k), yy(k - 2)
        for j, w, buf, ss, rs, to, t, has in (
            (b_up[i], wu, ub, ub_s, ub_r, yup, 0, k > 1 or b_up[i] < 4),
            (b_dn[i], wd, db, db_s, db_r, ydn, 1, k > 1 or b_dn[i] >= 4),
        ):
            n = 8 * (k - 1) + j
            if has:
                arrived(buf.at[k - 1, j], ss.at[n], rs.at[n])
                blend(mb.at[w, j], buf.at[k - 1, j], turned(b_wt[k][t], HR * j))
            if k < 2:
                send(mb.at[w, j], buf.at[k, j], ss.at[n + 8], rs.at[n + 8], to)

    def a_y():
        for d in (1, 2, 3):
            w = yy(d)
            send(sa.at[z], ysa.at[d - 1], ysa_s.at[d - 1], ysa_r.at[d - 1], pid(y + d, z, c))
            send(ma.at[z, w], ya.at[d - 1], ya_s.at[d - 1], ya_r.at[d - 1], pid(y + d, z, c))

    def a_y_end():
        total = turned(sa[z], HR * y)
        for d in (1, 3, 2):
            arrived(ysa.at[d - 1], ysa_s.at[d - 1], ysa_r.at[d - 1])
            total, wt = join(total, turned(ysa[d - 1], HR * y))
            arrived(ya.at[d - 1], ya_s.at[d - 1], ya_r.at[d - 1])
            blend(ma.at[z, y], ya.at[d - 1], wt)

    def bz_first():
        w = zz(4)
        usz[4] = turned(sb[y], HR * w)
        send(usz.at[4], usz.at[0], usz_s.at[0], usz_r.at[0], zup)
        send(usz.at[4], dsz.at[0], dsz_s.at[0], dsz_r.at[0], zdn)
        lo, hi = pl.ds(0, HR // 2), pl.ds(HR // 2, HR // 2)
        send(mb.at[y, w, lo], uz.at[0, lo], uz_s.at[0], uz_r.at[0], zup)
        send(mb.at[y, w, hi], dz.at[0, hi], dz_s.at[0], dz_r.at[0], zdn)

    def bz_step(k):
        wu, wd = zz(4 - k), zz(k - 4)
        lo, hi = pl.ds(0, HR // 2), pl.ds(HR // 2, HR // 2)
        arrived(usz.at[k - 1], usz_s.at[k - 1], usz_r.at[k - 1])
        ru = usz[k - 1]
        if k == 1:
            ru = jnp.where(lane < HR // 2, ru, NEG)
        newu, wtu = join(turned(sb[y], HR * wu), ru)
        if k < 4:
            usz[4 + k] = newu
            send(usz.at[4 + k], usz.at[k], usz_s.at[k], usz_r.at[k], zup)
        arrived(dsz.at[k - 1], dsz_s.at[k - 1], dsz_r.at[k - 1])
        rd = dsz[k - 1]
        if k == 1:
            rd = jnp.where(lane < HR // 2, NEG, rd)
        own = turned(sb[y], HR * wd) if k < 4 else newu
        newd, wtd = join(own, rd)
        if k < 4:
            dsz[4 + k] = newd
            send(dsz.at[4 + k], dsz.at[k], dsz_s.at[k], dsz_r.at[k], zdn)
        if k == 1:
            arrived(uz.at[0, lo], uz_s.at[0], uz_r.at[0])
            blend(mb.at[y, wu], uz.at[0], wtu, HR // 2, 0)
        else:
            arrived(uz.at[k - 1], uz_s.at[k - 1], uz_r.at[k - 1])
            blend(mb.at[y, wu], uz.at[k - 1], wtu)
        if k < 4:
            send(mb.at[y, wu], uz.at[k], uz_s.at[k], uz_r.at[k], zup)
        if k == 1:
            arrived(dz.at[0, hi], dz_s.at[0], dz_r.at[0])
            blend(mb.at[y, wd], dz.at[0], wtd, HR // 2, HR // 2)
        else:
            arrived(dz.at[k - 1], dz_s.at[k - 1], dz_r.at[k - 1])
            blend(mb.at[y, wd], dz.at[k - 1], wtd)
        if k < 4:
            send(mb.at[y, wd], dz.at[k], dz_s.at[k], dz_r.at[k], zdn)

    def share(h, cell):
        fa[...] = cell[...].astype(jnp.float32).reshape(HR * 16, HD)
        for i in range(16):
            near[h, y, :, i * HD:(i + 1) * HD] = fa[pl.ds(i, HR, stride=16), :].astype(jnp.bfloat16)
        for d in (1, 2, 3):
            n = 3 * h + d - 1
            send(near.at[h, y], near.at[h, y], n_s.at[n], n_r.at[n], pid(y + d, z, c))

    def project():
        for h in (0, 1):
            for d in (1, 3, 2):
                n = 3 * h + d - 1
                arrived(near.at[h, yy(-d)], n_s.at[n], n_r.at[n])
        rows = near[...].reshape(2 * NY * HR, near.shape[-1])
        wide = w_ref.shape[0]
        for lo in range(0, wide, 256):
            t = lax.dot_general(rows, w_ref[lo:lo + 256, :], (((1,), (1,)), ((), ())), preferred_element_type=jnp.float32)
            terms[:, :, :, lo:lo + 256] = t.astype(jnp.bfloat16).reshape(2, NY, HR, 256)
        for h in (0, 1):
            for d in (1, 2, 3):
                n = 3 * h + d - 1
                to = (x + d) % NX
                send(terms.at[h, to], xin.at[h, d - 1], t_s.at[n], t_r.at[n], me, to)

    def finish(h):
        total = terms[h, x].astype(jnp.float32)
        for d in (1, 3, 2):
            n = 3 * h + d - 1
            arrived(xin.at[h, d - 1], t_s.at[n], t_r.at[n])
            total += xin[h, d - 1].astype(jnp.float32)
        tsum[h] = total.astype(jnp.bfloat16)

        @pl.when(x != y)
        def _():
            pltpu.make_async_remote_copy(src_ref=tsum.at[h], dst_ref=fin.at[h], send_sem=g_s.at[h], recv_sem=g_r.at[h], device_id=flip, device_id_type=MESH).start()

    def land(h):
        @pl.when(x != y)
        def _():
            pltpu.make_async_remote_copy(src_ref=tsum.at[h], dst_ref=fin.at[h], send_sem=g_s.at[h], recv_sem=g_r.at[h], device_id=flip, device_id_type=MESH).wait()
            out_ref[pl.ds(h * HR, HR)] = fin[h]

        @pl.when(x == y)
        def _():
            out_ref[pl.ds(h * HR, HR)] = tsum[h]

    core_a(0)
    a_first()
    core_b(0)
    b_first()
    core_a(1)
    core_a(2)
    a_cell(1, 0)
    a_cell(1, 1)
    core_b(1)
    core_b(2)
    for i in range(4):
        b_cell(1, i)
    a_stat(1)
    a_cell(1, 2)
    a_cell(1, 3)
    core_a(3)
    core_a(4)
    b_stat(1)
    a_stat(2)
    for i in range(4):
        a_cell(2, i)
        b_cell(1, 4 + i)
    core_a(5)
    core_a(6)
    a_stat(3)
    core_b(3)
    b_stat(2)
    for i in range(4):
        a_cell(3, i)
        b_cell(2, i)
    core_a(7)
    a_stat(4)
    for i in range(4):
        b_cell(2, 4 + i)
        if i == 3:
            bz_first()
        a_cell(4, i)
    bz_step(1)
    a_y()
    bz_step(2)
    a_y_end()
    share(0, ma.at[z, y])
    bz_step(3)
    bz_step(4)
    share(1, mb.at[y, z])
    project()
    finish(0)
    finish(1)
    land(0)
    land(1)
    for d in sends:
        d.wait_send()


def merge(d, st, weight):
    dma = pltpu.SemaphoreType.DMA
    bf, f32 = jnp.bfloat16, jnp.float32

    def v(*shape, dtype=bf):
        return pltpu.VMEM(shape + (16, 128), dtype)

    anyspec = pl.BlockSpec(memory_space=pl.ANY)
    vmem = pl.BlockSpec(memory_space=pltpu.VMEM)
    sems = [6, 6, 6, 6, 2, 2]
    sems += [2, 14, 14, 16, 16, 16, 16, 4, 4, 4, 4, 16, 16, 16, 16, 2, 2, 2, 2, 3, 3, 3, 3, 4, 4, 4, 4, 4, 4, 4, 4]
    wide, deep = weight.shape
    return pl.pallas_call(
        merge_kernel,
        out_shape=jax.ShapeDtypeStruct((2 * HR, wide), bf),
        in_specs=[vmem, vmem, vmem],
        out_specs=vmem,
        scratch_shapes=[
            v(NZ, NY, HR), v(NY, NZ, HR), v(NZ, NY * HR), v(NY, NZ * HR),
            v(NZ, dtype=f32), v(NY, dtype=f32), v(NZ, dtype=f32), v(NY, dtype=f32),
            v(4, NY, HR), v(4, NY, HR), v(5, dtype=f32), v(5, dtype=f32),
            v(2, NZ, HR), v(2, NZ, HR), v(3, dtype=f32), v(3, dtype=f32),
            v(3, HR), v(3, dtype=f32),
            v(4, HR), v(4, HR), v(8, dtype=f32), v(8, dtype=f32),
            pltpu.VMEM((HR * 16, HD), f32),
            pltpu.VMEM((2, NY, HR, deep), bf),
            pltpu.VMEM((2, NY, HR, wide), bf),
            pltpu.VMEM((2, 3, HR, wide), bf),
            pltpu.VMEM((2, HR, wide), bf),
            pltpu.VMEM((2, HR, wide), bf),
        ] + [dma((n,)) for n in sems],
        compiler_params=pltpu.CompilerParams(collective_id=1, has_side_effects=True, vmem_limit_bytes=20 * 2**20),
        name="merge",
    )(d, st, pltpu.with_memory_space_constraint(weight, pltpu.VMEM))


def body(queries, span_keys, span_values, span_ids, span_slot, out_weight):
    rows, width = queries.shape
    qs, ws, last = gather(with_ids(queries.reshape(rows, width // HD, HD), span_ids), out_weight.T)
    d, st = attend(last, span_slot, qs, span_keys, span_values)
    return merge(d, st, ws.reshape(-1, width))


def solution(mesh):
    in_specs = (
        P("pool", "head"),
        P("pool", None, "head"),
        P("pool", None, "head"),
        P("pool", None),
        P(),
        P("head", "pool"),
    )
    return jax.shard_map(body, mesh=mesh, in_specs=in_specs, out_specs=P("pool", "head"), check_vma=False)
```
